32 devices in a mesh: tm: 8 (over z, core), space: 4 (over y, x).
Axes of the slice: x: 2, y: 2, z: 4, core: 2. Of those that a mesh axis runs over, the one named last changes fastest.
Arguments:
- slab_starts: float32 [8, 4, 4, 4, 32, 128], P('tm', None, None, None, 'space'), may hold values from -1.4 to 6, as said below
- coarse_factor: float32 [4, 32, 128], P(None, 'space'), may hold values from 0.2 to 1
- blend_weight: float32 [32, 128], P('space'), may hold values from 0.2 to 0.9
- blend_flags: int32 [32, 128], P('space'), may hold values 0 or 1
Outputs:
- slab_ends: float32 [8, 4, 4, 4, 32, 128], P('tm', None, None, None, 'space')
- jump_norm: float32 [8], P('tm')
The draws below stay inside these ranges and needn't reach their ends.
Inputs may be any that keep to these rules, and one draw needn't show every extreme that they name: `slab_starts`: at every node the density and the pressure lie between 0.5 and 2 and each velocity component between -0.7 and 0.7.
All inputs are finite; a program needn't handle non-finite values. No bound on the sum of `blend_flags` on one device may be relied on, other than what follows from the above.
Results may differ from the reference program's by a relative error of at most 0.0003.
Values sent between devices are 32-bit elements; how exact they have to be, the bound alone decides.
A program may use at most 128 MiB of HBM per device.

```python
import math
import jax
import jax.numpy as jnp
import numpy as np
from jax import lax

VARS = 4
NODES = 4
FSTEPS = 4
EY = 128
SLABS = 8
NX = 32


def draw_slab_starts(key, part):
    grid_shape = (SLABS, NODES, NODES, NX, EY)
    subkeys = jax.random.split(jax.random.fold_in(key, 17), 4)
    density = jnp.exp(jax.random.uniform(subkeys[0], grid_shape, jnp.float32, math.log(0.5), math.log(2.0)))
    pressure = jnp.exp(jax.random.uniform(subkeys[1], grid_shape, jnp.float32, math.log(0.5), math.log(2.0)))
    velocity_x = jnp.clip(0.3 * jax.random.normal(subkeys[2], grid_shape, jnp.float32), -0.7, 0.7)
    velocity_y = jnp.clip(0.3 * jax.random.normal(subkeys[3], grid_shape, jnp.float32), -0.7, 0.7)
    energy = pressure / 0.4 + 0.5 * density * (velocity_x * velocity_x + velocity_y * velocity_y)
    return jnp.stack([density, density * velocity_x, density * velocity_y, energy], axis=1)


def place_ends(result, key, low, top_value):
    longest = result.shape.index(max(result.shape))
    spots = []
    for shift in (0, 1):
        where = [jax.random.randint(jax.random.fold_in(key, axis), (), 0, length) for axis, length in enumerate(result.shape)]
        where[longest] = (where[longest] + shift) % result.shape[longest]
        spots.append(tuple(where))
    return result.at[spots[0]].set(low).at[spots[1]].set(top_value)


def level_of(stream_key, shape, pieces, low, high):
    level = 1.0
    for axis_at, parts in pieces:
        heights = jax.random.uniform(jax.random.fold_in(jax.random.fold_in(stream_key, 6), axis_at), (parts,), jnp.float32, low / len(pieces), high / len(pieces))
        level = level * jnp.repeat(jnp.exp(heights), shape[axis_at] // parts).reshape((-1,) + (1,) * (len(shape) - 1 - axis_at))
    return level


def setup_inputs(seed: int = 0) -> dict:
    arg_keys = jax.random.split(jax.random.key(seed), 5)
    slab_starts = draw_slab_starts(jax.random.fold_in(arg_keys[4], 71), 0)
    coarse_factor = jnp.clip(jnp.exp(math.log(1.0) - 1.609438 * jax.random.uniform(arg_keys[1], (VARS, NX, EY), jnp.float32) ** level_of(arg_keys[1], (VARS, NX, EY), ((1, 4),), -0.2, 0.2)), 0.2, 1.0)
    blend_weight = jnp.clip(0.2 + 0.7 * jax.random.uniform(arg_keys[2], (NX, EY), jnp.float32) ** level_of(arg_keys[2], (NX, EY), ((0, 4),), -0.2, 0.2), 0.2, 0.9)
    blend_flags = place_ends((jax.random.randint(arg_keys[3], (NX, EY), 0, 2) < 1).astype(jnp.int32), jax.random.fold_in(arg_keys[3], 1), 0, 1)
    return {"slab_starts": slab_starts, "coarse_factor": coarse_factor, "blend_weight": blend_weight, "blend_flags": blend_flags}


gamma_ratio = 1.4
step_size = 0.003

def tables():
    inner = 1.0 / math.sqrt(5.0)
    points = np.array([-1.0, -inner, inner, 1.0])
    weights = np.array([1.0 / 6.0, 5.0 / 6.0, 5.0 / 6.0, 1.0 / 6.0])
    scales = np.array([1.0 / np.prod([points[column] - points[others] for others in range(4) if others != column]) for column in range(4)])
    derivative = np.zeros((4, 4))
    for row_index in range(4):
        for col_index in range(4):
            if row_index != col_index:
                derivative[row_index, col_index] = scales[col_index] / scales[row_index] / (points[row_index] - points[col_index])
        derivative[row_index, row_index] = -np.sum(derivative[row_index])
    return (jnp.asarray(derivative, dtype=jnp.float32), jnp.asarray(weights, dtype=jnp.float32))

def primitives(state):
    density = state[0]
    velocity_x = state[1] / density
    velocity_y = state[2] / density
    pressure = (gamma_ratio - 1.0) * (state[3] - 0.5 * density * (velocity_x * velocity_x + velocity_y * velocity_y))
    return (density, velocity_x, velocity_y, pressure)

def log_terms(left, right):
    ratio = (left * (left - 2.0 * right) + right * right) / (left * (left + 2.0 * right) + right * right)
    series = 105.0 + ratio * (35.0 + ratio * (21.0 + ratio * 15.0))
    nearly = ratio < 0.0001
    safe_left = jnp.where(nearly, 1.0, left)
    safe_right = jnp.where(nearly, 2.0, right)
    return (nearly, series, jnp.log(safe_right / safe_left), safe_right - safe_left)

def log_mean(left, right):
    nearly, series, logged, differ = log_terms(left, right)
    return jnp.where(nearly, (left + right) * 52.5 / series, differ / logged)

def inverse_log_mean(left, right):
    nearly, series, logged, differ = log_terms(left, right)
    return jnp.where(nearly, series / (52.5 * (left + right)), logged / differ)

def entropy_flux(left, right):
    density_left, normal_left, along_left, pressure_left = left
    density_right, normal_right, along_right, pressure_right = right
    mass_mean = log_mean(density_left, density_right)
    normal_mean = 0.5 * (normal_left + normal_right)
    along_mean = 0.5 * (along_left + along_right)
    pressure_mean = 0.5 * (pressure_left + pressure_right)
    thermal = pressure_left * pressure_right * inverse_log_mean(density_left * pressure_right, density_right * pressure_left)
    kinetic = 0.5 * (normal_left * normal_right + along_left * along_right)
    mass_flux = mass_mean * normal_mean
    normal_flux = mass_flux * normal_mean + pressure_mean
    along_flux = mass_flux * along_mean
    energy_flux = mass_flux * (kinetic + thermal / (gamma_ratio - 1.0)) + 0.5 * (pressure_left * normal_right + pressure_right * normal_left)
    return (mass_flux, normal_flux, along_flux, energy_flux)

def physical_flux(prims):
    density, normal, along, pressure = prims
    mass_flux = density * normal
    energy_total = pressure / (gamma_ratio - 1.0) + 0.5 * density * (normal * normal + along * along)
    return (mass_flux, mass_flux * normal + pressure, mass_flux * along, normal * (energy_total + pressure))

def oriented(prims, axis):
    density, velocity_x, velocity_y, pressure = prims
    if axis == 1:
        return (density, velocity_x, velocity_y, pressure)
    return (density, velocity_y, velocity_x, pressure)

def restack(fluxes, axis):
    mass_flux, normal_flux, along_flux, energy_flux = fluxes
    if axis == 1:
        return jnp.stack([mass_flux, normal_flux, along_flux, energy_flux], 0)
    return jnp.stack([mass_flux, along_flux, normal_flux, energy_flux], 0)

def wave_speed(prims):
    density, normal, along, pressure = prims
    return jnp.abs(normal) + jnp.sqrt(gamma_ratio * pressure / density)

def rusanov(state_left, state_right, axis, central):
    prims_left = oriented(primitives(state_left), axis)
    prims_right = oriented(primitives(state_right), axis)
    if central:
        centre = restack(entropy_flux(prims_left, prims_right), axis)
    else:
        centre = 0.5 * (restack(physical_flux(prims_left), axis) + restack(physical_flux(prims_right), axis))
    speed = jnp.maximum(wave_speed(prims_left), wave_speed(prims_right))
    return centre - 0.5 * speed * (state_right - state_left)

def direction_rate(state, axis, face_left, face_right, blend, derivative, weights):
    prims = oriented(primitives(state), axis)
    node = axis - 1
    rows = tuple((jnp.expand_dims(field, node + 1) for field in prims))
    columns = tuple((jnp.expand_dims(field, node) for field in prims))
    pairs = restack(entropy_flux(rows, columns), axis)
    table_shape = [1, 1, 1, 1, 1, 1]
    table_shape[axis] = 4
    table_shape[axis + 1] = 4
    volume = lax.optimization_barrier(jnp.sum((2.0 * derivative).reshape(table_shape) * pairs, axis=axis + 1))
    physical = restack(physical_flux(prims), axis)
    lower = (face_left - jnp.take(physical, 0, axis=axis)) / weights[0]
    upper = (face_right - jnp.take(physical, 3, axis=axis)) / weights[3]
    middle = jnp.zeros_like(lax.slice_in_dim(physical, 1, 3, axis=axis))
    boundary = jnp.concatenate([-jnp.expand_dims(lower, axis), middle, jnp.expand_dims(upper, axis)], axis)
    galerkin = -2.0 * (volume + boundary)
    inner_flux = rusanov(lax.slice_in_dim(state, 0, 3, axis=axis), lax.slice_in_dim(state, 1, 4, axis=axis), axis, False)
    walls = jnp.concatenate([jnp.expand_dims(face_left, axis), inner_flux, jnp.expand_dims(face_right, axis)], axis)
    weight_shape = [1, 1, 1, 1, 1]
    weight_shape[axis] = 4
    subcell = -2.0 * (lax.slice_in_dim(walls, 1, 5, axis=axis) - lax.slice_in_dim(walls, 0, 4, axis=axis)) / weights.reshape(weight_shape)
    return (1.0 - blend) * galerkin + blend * subcell

def vertical_faces(state):
    lower_trace = state[:, :, 0]
    upper_trace = state[:, :, 3]
    behind = jnp.roll(upper_trace, 1, axis=3)
    face_left = rusanov(behind, lower_trace, 2, True)
    return (face_left, jnp.roll(face_left, -1, axis=3))

def rolled_faces(state):
    lower_trace = state[:, 0]
    upper_trace = state[:, 3]
    behind = jnp.roll(upper_trace, 1, axis=2)
    face_left = rusanov(behind, lower_trace, 1, True)
    return (face_left, jnp.roll(face_left, -1, axis=2))

def rate(state, blend, derivative, weights, horizontal):
    face_left, face_right = horizontal(state)
    across = direction_rate(state, 1, face_left, face_right, blend, derivative, weights)
    face_low, face_high = vertical_faces(state)
    upward = direction_rate(state, 2, face_low, face_high, blend, derivative, weights)
    return across + upward

def fine_slab(state, blend, derivative, weights, horizontal):
    for repeat_index in range(FSTEPS):
        section = state + step_size * rate(state, blend, derivative, weights, horizontal)
        state = 0.5 * state + 0.5 * (section + step_size * rate(section, blend, derivative, weights, horizontal))
    return state

def quadrature_table(weights):
    return (weights[:, None] * weights[None, :] / 4.0).reshape(1, 4, 4, 1, 1)

def coarse(state, factor, quadrature):
    average = lax.optimization_barrier(jnp.sum(state * quadrature, axis=(1, 2), keepdims=True))
    return average + factor * (state - average)

def reference(slab_starts, coarse_factor, blend_weight, blend_flags):
    derivative, weights = tables()
    quadrature = quadrature_table(weights)
    blend = blend_flags.astype(jnp.float32) * blend_weight
    factor = coarse_factor[:, None, None]

    def advance_fine(opening):
        return fine_slab(opening, blend, derivative, weights, rolled_faces)
    fine_ends = lax.map(advance_fine, slab_starts)
    corrections = fine_ends - jax.vmap(lambda opening: coarse(opening, factor, quadrature))(slab_starts)

    def advance(carried, correction):
        closing = coarse(carried, factor, quadrature) + correction
        return (closing, (carried, closing))
    unused, (new_starts, slab_ends) = lax.scan(advance, slab_starts[0], corrections)
    jumps = new_starts - slab_starts
    totals = lax.optimization_barrier(jnp.sum(quadrature[None] * jumps * jumps, axis=(1, 2, 3, 4, 5)))
    jump_norm = jnp.sqrt(totals / (NX * EY))
    return (slab_ends, jump_norm)
```

```python
import functools
import math

import jax
import jax.numpy as jnp
import numpy as np
from jax import lax
from jax.experimental import pallas as pl
from jax.experimental.pallas import tpu as pltpu
from jax.sharding import PartitionSpec as P

FSTEPS = 4
NODES = 4
VARS = 4

gamma_ratio = 1.4
step_size = 0.003
MESH = pl.DeviceIdType.MESH


def tables():
    inner = 1.0 / math.sqrt(5.0)
    points = np.array([-1.0, -inner, inner, 1.0])
    weights = np.array([1.0 / 6.0, 5.0 / 6.0, 5.0 / 6.0, 1.0 / 6.0])
    scales = [
        1.0 / np.prod([points[c] - points[k] for k in range(4) if k != c]) for c in range(4)
    ]
    derivative = np.zeros((4, 4))
    for r in range(4):
        for c in range(4):
            if r != c:
                derivative[r, c] = scales[c] / scales[r] / (points[r] - points[c])
    return derivative, weights


DERIVATIVE, WEIGHTS = tables()
QUAD = [[float(WEIGHTS[i] * WEIGHTS[j] / 4.0) for j in range(4)] for i in range(4)]


def rough(x):
    return pl.reciprocal(x, approx=True)


def inverse(x):
    r = pl.reciprocal(x, approx=True)
    return r * (2.0 - x * r)


def near_terms(a, b):
    total = a + b
    differ = b - a
    ratio = differ * rough(total)
    ratio = ratio * ratio
    series = 2.0 + ratio * (35.0 / 52.5 + ratio * (21.0 / 52.5 + ratio * (15.0 / 52.5)))
    return ratio < 0.0001, total, differ, series


def node_fields(u):
    rho, mx, my, energy = u
    ir = inverse(rho)
    vx = mx * ir
    vy = my * ir
    p = 0.4 * energy - 0.2 * (mx * vx + my * vy)
    beta = rho * inverse(p)
    warm = gamma_ratio * p * ir
    sound = warm * lax.rsqrt(warm)
    return (vx, vy, p, beta, jnp.log(rho), 2.5 * jnp.log(beta), sound)


def two_point(left, right, axis, scale):
    (ul, fl), (ur, fr) = left, right
    vnl, vtl = (fl[0], fl[1]) if axis == 0 else (fl[1], fl[0])
    vnr, vtr = (fr[0], fr[1]) if axis == 0 else (fr[1], fr[0])
    near, total, differ, series = near_terms(ul[0], ur[0])
    mean = jnp.where(near, total, differ) * inverse(jnp.where(near, series, fr[4] - fl[4]))
    near, total, differ, series = near_terms(fl[3], fr[3])
    thermal = jnp.where(near, 2.5 * series, fr[5] - fl[5]) * inverse(
        jnp.where(near, total, differ)
    )
    half_n = 0.5 * (vnl + vnr)
    half_t = 0.5 * (vtl + vtr)
    mass = mean * half_n
    if scale != 1.0:
        mass = mass * scale
    normal = mass * half_n + (0.5 * scale) * (fl[2] + fr[2])
    along = mass * half_t
    energy = mass * (0.5 * (vnl * vnr + vtl * vtr) + thermal) + (0.5 * scale) * (
        fl[2] * vnr + fr[2] * vnl
    )
    return (mass, normal, along, energy) if axis == 0 else (mass, along, normal, energy)


def face_flux(left, right, axis):
    (ul, fl), (ur, fr) = left, right
    centre = two_point(left, right, axis, 1.0)
    speed = 0.5 * jnp.maximum(jnp.abs(fl[axis]) + fl[6], jnp.abs(fr[axis]) + fr[6])
    return [centre[v] - speed * (ur[v] - ul[v]) for v in range(VARS)]


def physical(node, axis):
    u, f = node
    vn = f[axis]
    flux = [u[0] * vn, u[1] * vn, u[2] * vn, (u[3] + f[2]) * vn]
    flux[0] = u[1 + axis]
    flux[1 + axis] = flux[1 + axis] + f[2]
    return flux


def line_fluxes(nodes, axis, blend):
    pair = {}
    for a in range(4):
        for b in range(a + 1, 4):
            weight = float(2.0 * WEIGHTS[a] * DERIVATIVE[a, b])
            pair[a, b] = two_point(nodes[a], nodes[b], axis, weight)
    phys = [physical(node, axis) for node in nodes]
    fast = [jnp.abs(node[1][axis]) + node[1][6] for node in nodes]
    speeds = [jnp.maximum(fast[k], fast[k + 1]) for k in range(3)]
    result = [[], [], []]
    for v in range(VARS):
        far = pair[0, 3][v]
        head = pair[0, 2][v] + far
        tail = pair[1, 3][v]
        high = [pair[0, 1][v] + head, head + (pair[1, 2][v] + tail), (far + tail) + pair[2, 3][v]]
        for k in range(3):
            low = 0.5 * (
                (phys[k][v] + phys[k + 1][v])
                - speeds[k] * (nodes[k + 1][0][v] - nodes[k][0][v])
            )
            result[k].append(high[k] + blend * (low - high[k]))
    return result


def rolled(node, shift, axis):
    return tuple(tuple(pltpu.roll(x, shift, axis) for x in part) for part in node)


def coarse(u, factor):
    mean = None
    for i in range(4):
        for j in range(4):
            term = QUAD[i][j] * u[i][j]
            mean = term if mean is None else mean + term
    return [[mean + factor * (u[i][j] - mean) for j in range(4)] for i in range(4)]


def kernel(
    n_space,
    n_tm,
    o_ref,
    fac_ref,
    bw_ref,
    bf_ref,
    end_ref,
    norm_ref,
    st,
    fld,
    acc,
    blend_ref,
    low_ref,
    high_ref,
    from_left,
    from_right,
    edge_ref,
    corr,
    mate,
    pairs,
    start_ref,
    jump_ref,
    halo_send,
    halo_recv,
    corr_send,
    corr_recv,
    chain_send,
    chain_recv,
    fwd_send,
    fwd_recv,
    jump_send,
    jump_recv,
):
    rows, lanes = bw_ref.shape
    sp = lax.axis_index("space")
    tm = lax.axis_index("tm")
    core = lax.rem(tm, 2)
    z = lax.div(tm, 2)
    partner = tm + 1 - 2 * core
    chips = n_tm // 2
    left = lax.rem(sp + n_space - 1, n_space)
    right = lax.rem(sp + 1, n_space)
    takes = jnp.logical_and(core == 1, z > 0)
    gives = jnp.logical_and(core == 1, z < chips - 1)

    barrier = pltpu.get_barrier_semaphore()
    for k in range(1, n_space):
        other = lax.rem(sp + k, n_space)
        pl.semaphore_signal(barrier, inc=1, device_id={"space": other}, device_id_type=MESH)
    pl.semaphore_signal(barrier, inc=1, device_id={"tm": partner}, device_id_type=MESH)

    @pl.when(takes)
    def _():
        pl.semaphore_signal(barrier, inc=1, device_id={"tm": tm - 2}, device_id_type=MESH)

    @pl.when(gives)
    def _():
        pl.semaphore_signal(barrier, inc=1, device_id={"tm": tm + 2}, device_id_type=MESH)

    blend_ref[...] = bf_ref[...].astype(jnp.float32) * bw_ref[...]
    for v in range(VARS):
        for j in range(4):
            low = o_ref[0, v, 0, j, 0:1, :]
            high = o_ref[0, v, 3, j, rows - 1 : rows, :]
            for base in (0, 4):
                low_ref[0, v, base + j : base + j + 1, :] = low
                high_ref[0, v, base + j : base + j + 1, :] = high
    st[0] = o_ref[0]

    peers = n_space + takes.astype(jnp.int32) + gives.astype(jnp.int32)
    pl.semaphore_wait(barrier, peers)

    def halo(slot):
        return (
            pltpu.make_async_remote_copy(
                src_ref=low_ref.at[slot],
                dst_ref=from_right.at[slot],
                send_sem=halo_send.at[slot, 0],
                recv_sem=halo_recv.at[slot, 0],
                device_id={"space": left},
                device_id_type=MESH,
            ),
            pltpu.make_async_remote_copy(
                src_ref=high_ref.at[slot],
                dst_ref=from_left.at[slot],
                send_sem=halo_send.at[slot, 1],
                recv_sem=halo_recv.at[slot, 1],
                device_id={"space": right},
                device_id_type=MESH,
            ),
        )

    for copy in halo(0):
        copy.start()

    row_at = lax.broadcasted_iota(jnp.int32, (rows, lanes), 0)
    first_row = row_at == 0
    last_row = row_at == rows - 1
    upper_half = lax.broadcasted_iota(jnp.int32, (8, lanes), 0) < 4
    gain = [float(-2.0 / WEIGHTS[i]) for i in range(4)]

    def stage(s, _):
        now = lax.rem(s, 2)
        later = 1 - now
        keep = 0.5 * now.astype(jnp.float32)
        fresh = 1.0 - keep
        fresh_step = fresh * step_size

        def load(i, j):
            u = tuple(st[now, v, i, j] for v in range(VARS))
            return (u, tuple(fld[k, i, j] for k in range(7)))

        def fill(t, _):
            for j in range(4):
                values = node_fields(tuple(st[now, v, t, j] for v in range(VARS)))
                for k in range(7):
                    fld[k, t, j] = values[k]
            return 0

        lax.fori_loop(0, 4, fill, 0)

        def across(t, _):
            nodes = [load(i, t) for i in range(4)]
            inner = line_fluxes(nodes, 0, blend_ref[...])
            face = face_flux(rolled(nodes[3], 1, 0), nodes[0], 0)
            for v in range(VARS):
                lower = jnp.where(first_row, 0.0, face[v])
                upper = jnp.where(last_row, 0.0, pltpu.roll(face[v], rows - 1, 0))
                walls = [lower, inner[0][v], inner[1][v], inner[2][v], upper]
                for i in range(4):
                    acc[v, i, t] = gain[i] * (walls[i + 1] - walls[i])
            return 0

        lax.fori_loop(0, 4, across, 0)

        def upward(t, _):
            nodes = [load(t, j) for j in range(4)]
            inner = line_fluxes(nodes, 1, blend_ref[...])
            face = face_flux(rolled(nodes[3], 1, 1), nodes[0], 1)
            for v in range(VARS):
                upper = pltpu.roll(face[v], lanes - 1, 1)
                walls = [face[v], inner[0][v], inner[1][v], inner[2][v], upper]
                for j in range(4):
                    total = acc[v, t, j] + gain[j] * (walls[j + 1] - walls[j])
                    st[later, v, t, j] = (
                        keep * st[0, v, t, j] + fresh * nodes[j][0][v] + fresh_step * total
                    )
            return 0

        lax.fori_loop(0, 4, upward, 0)

        copies = halo(now)
        for copy in copies:
            copy.wait()

        uleft = tuple(
            jnp.where(upper_half, from_left[now, v], high_ref[now, v]) for v in range(VARS)
        )
        uright = tuple(
            jnp.where(upper_half, low_ref[now, v], from_right[now, v]) for v in range(VARS)
        )
        edge = face_flux((uleft, node_fields(uleft)), (uright, node_fields(uright)), 0)
        factor = jnp.where(upper_half, -gain[0] * fresh_step, gain[3] * fresh_step)
        for v in range(VARS):
            edge_ref[v] = factor * edge[v]
        for v in range(VARS):
            for j in range(4):
                low = st[later, v, 0, j, 0:1, :] + edge_ref[v, j : j + 1, :]
                high = st[later, v, 3, j, rows - 1 : rows, :] + edge_ref[v, 4 + j : 5 + j, :]
                st[later, v, 0, j, 0:1, :] = low
                st[later, v, 3, j, rows - 1 : rows, :] = high
                for base in (0, 4):
                    low_ref[later, v, base + j : base + j + 1, :] = low
                    high_ref[later, v, base + j : base + j + 1, :] = high

        @pl.when(s < 2 * FSTEPS - 1)
        def _():
            for copy in halo(later):
                copy.start()

        return 0

    lax.fori_loop(0, 2 * FSTEPS, stage, 0)

    def grid_of(view):
        return [[view(i, j) for j in range(4)] for i in range(4)]

    def pass_on(src, dst, send, recv, v, device):
        return pltpu.make_async_remote_copy(
            src_ref=src.at[v],
            dst_ref=dst.at[v],
            send_sem=send.at[v],
            recv_sem=recv.at[v],
            device_id={"tm": device},
            device_id_type=MESH,
        )

    def to_mate(v):
        return pass_on(corr, mate, corr_send, corr_recv, v, partner)

    def to_next(v):
        return pass_on(end_ref.at[0], start_ref, chain_send, chain_recv, v, tm + 2)

    def to_first(v):
        return pass_on(start_ref, start_ref, fwd_send, fwd_recv, v, partner)

    counted = jnp.where(tm == 0, 0.0, 1.0)
    for v in range(VARS):
        base = coarse(grid_of(lambda i, j: o_ref[0, v, i, j]), fac_ref[v])
        for i in range(4):
            for j in range(4):
                corr[v, i, j] = st[0, v, i, j] - counted * base[i][j]

        @pl.when(core == 0)
        def _():
            to_mate(v).start()

    jump_ref[0] = jnp.zeros((rows, lanes), jnp.float32)

    @pl.when(core == 0)
    def _():
        @pl.when(z == 0)
        def _():
            end_ref[0] = corr[...]

        @pl.when(z > 0)
        def _():
            total = jnp.zeros((rows, lanes), jnp.float32)
            for v in range(VARS):
                to_first(v).wait_recv()
                begun = grid_of(lambda i, j: start_ref[v, i, j])
                ended = coarse(begun, fac_ref[v])
                for i in range(4):
                    for j in range(4):
                        jump = begun[i][j] - o_ref[0, v, i, j]
                        total = total + QUAD[i][j] * (jump * jump)
                        end_ref[0, v, i, j] = ended[i][j] + corr[v, i, j]
            jump_ref[0] = total

        for v in range(VARS):
            to_mate(v).wait_send()

    @pl.when(core == 1)
    def _():
        @pl.when(z == 0)
        def _():
            start_ref[...] = jnp.zeros_like(start_ref)

        for v in range(VARS):
            to_mate(v).wait_recv()
            half = coarse(grid_of(lambda i, j: mate[v, i, j]), fac_ref[v])
            for i in range(4):
                for j in range(4):
                    pairs[v, i, j] = half[i][j] + corr[v, i, j]

        for v in range(VARS):

            @pl.when(z > 0)
            def _():
                to_next(v).wait_recv()
                to_first(v).start()

            factor = fac_ref[v]
            ended = coarse(grid_of(lambda i, j: start_ref[v, i, j]), factor * factor)
            for i in range(4):
                for j in range(4):
                    end_ref[0, v, i, j] = ended[i][j] + pairs[v, i, j]

            @pl.when(gives)
            def _():
                to_next(v).start()

        total = jnp.zeros((rows, lanes), jnp.float32)
        for v in range(VARS):
            begun = coarse(grid_of(lambda i, j: start_ref[v, i, j]), fac_ref[v])
            for i in range(4):
                for j in range(4):
                    jump = (begun[i][j] + mate[v, i, j]) - o_ref[0, v, i, j]
                    total = total + QUAD[i][j] * (jump * jump)
        jump_ref[0] = total

    def share(k):
        return pltpu.make_async_remote_copy(
            src_ref=jump_ref.at[0],
            dst_ref=jump_ref.at[k],
            send_sem=jump_send.at[k],
            recv_sem=jump_recv.at[k],
            device_id={"space": lax.rem(sp + k, n_space)},
            device_id_type=MESH,
        )

    for k in range(1, n_space):
        share(k).start()

    @pl.when(takes)
    def _():
        for v in range(VARS):
            to_first(v).wait_send()

    @pl.when(gives)
    def _():
        for v in range(VARS):
            to_next(v).wait_send()

    for k in range(1, n_space):
        share(k).wait()
    total = jump_ref[0]
    for k in range(1, n_space):
        total = total + jump_ref[k]
    total = jnp.sum(jnp.sum(total, axis=0, keepdims=True), axis=1, keepdims=True)
    norm_ref[...] = jnp.broadcast_to(
        jnp.sqrt(total * (1.0 / (n_space * rows * lanes))), norm_ref.shape
    )


def solution(mesh):
    n_tm = mesh.shape["tm"]
    n_space = mesh.shape["space"]

    def on_device(slab_starts, coarse_factor, blend_weight, blend_flags):
        rows, lanes = blend_weight.shape
        state = (VARS, NODES, NODES, rows, lanes)
        f32 = jnp.float32
        dma = pltpu.SemaphoreType.DMA
        vmem = pl.BlockSpec(memory_space=pltpu.VMEM)
        edges = pltpu.VMEM((2, VARS, 8, lanes), f32)
        ends, norm = pl.pallas_call(
            functools.partial(kernel, n_space, n_tm),
            out_shape=(
                jax.ShapeDtypeStruct((1,) + state, f32),
                jax.ShapeDtypeStruct((1, 128), f32),
            ),
            in_specs=[vmem] * 4,
            out_specs=(vmem, vmem),
            scratch_shapes=[
                pltpu.VMEM((2,) + state, f32),
                pltpu.VMEM((7, NODES, NODES, rows, lanes), f32),
                pltpu.VMEM(state, f32),
                pltpu.VMEM((rows, lanes), f32),
                edges,
                edges,
                edges,
                edges,
                pltpu.VMEM((VARS, 8, lanes), f32),
                pltpu.VMEM(state, f32),
                pltpu.VMEM(state, f32),
                pltpu.VMEM(state, f32),
                pltpu.VMEM(state, f32),
                pltpu.VMEM((n_space, rows, lanes), f32),
                dma((2, 2)),
                dma((2, 2)),
                dma((VARS,)),
                dma((VARS,)),
                dma((VARS,)),
                dma((VARS,)),
                dma((VARS,)),
                dma((VARS,)),
                dma((n_space,)),
                dma((n_space,)),
            ],
            compiler_params=pltpu.CompilerParams(
                collective_id=0, has_side_effects=True, vmem_limit_bytes=32 * 1024 * 1024
            ),
        )(slab_starts, coarse_factor, blend_weight, blend_flags)
        return ends, norm[0, :1]

    in_specs = (
        P("tm", None, None, None, "space", None),
        P(None, "space", None),
        P("space", None),
        P("space", None),
    )
    out_specs = (P("tm", None, None, None, "space", None), P("tm"))
    return jax.shard_map(
        on_device, mesh=mesh, in_specs=in_specs, out_specs=out_specs, check_vma=False
    )
```

```python
import functools
import math

import jax
import jax.numpy as jnp
import numpy as np
from jax import lax
from jax.experimental import pallas as pl
from jax.experimental.pallas import tpu as pltpu
from jax.sharding import PartitionSpec as P

FSTEPS = 4
NODES = 4
VARS = 4

gamma_ratio = 1.4
step_size = 0.003
MESH = pl.DeviceIdType.MESH


def tables():
    inner = 1.0 / math.sqrt(5.0)
    points = np.array([-1.0, -inner, inner, 1.0])
    weights = np.array([1.0 / 6.0, 5.0 / 6.0, 5.0 / 6.0, 1.0 / 6.0])
    scales = [
        1.0 / np.prod([points[c] - points[k] for k in range(4) if k != c]) for c in range(4)
    ]
    derivative = np.zeros((4, 4))
    for r in range(4):
        for c in range(4):
            if r != c:
                derivative[r, c] = scales[c] / scales[r] / (points[r] - points[c])
    return derivative, weights


DERIVATIVE, WEIGHTS = tables()
QUAD = [[float(WEIGHTS[i] * WEIGHTS[j] / 4.0) for j in range(4)] for i in range(4)]


def rough(x):
    return pl.reciprocal(x, approx=True)


def inverse(x):
    r = pl.reciprocal(x, approx=True)
    return r * (2.0 - x * r)


def near_terms(a, b):
    total = a + b
    differ = b - a
    ratio = differ * rough(total)
    ratio = ratio * ratio
    series = 2.0 + ratio * (35.0 / 52.5 + ratio * (21.0 / 52.5 + ratio * (15.0 / 52.5)))
    return ratio < 0.0001, total, differ, series


def node_fields(u):
    rho, mx, my, energy = u
    ir = inverse(rho)
    vx = mx * ir
    vy = my * ir
    p = 0.4 * energy - 0.2 * (mx * vx + my * vy)
    beta = rho * inverse(p)
    warm = gamma_ratio * p * ir
    sound = warm * lax.rsqrt(warm)
    return (vx, vy, p, beta, jnp.log(rho), 2.5 * jnp.log(beta), sound)


def two_point(left, right, axis, scale):
    (ul, fl), (ur, fr) = left, right
    vnl, vtl = (fl[0], fl[1]) if axis == 0 else (fl[1], fl[0])
    vnr, vtr = (fr[0], fr[1]) if axis == 0 else (fr[1], fr[0])
    near, total, differ, series = near_terms(ul[0], ur[0])
    mean = jnp.where(near, total, differ) * inverse(jnp.where(near, series, fr[4] - fl[4]))
    near, total, differ, series = near_terms(fl[3], fr[3])
    thermal = jnp.where(near, 2.5 * series, fr[5] - fl[5]) * inverse(
        jnp.where(near, total, differ)
    )
    half_n = 0.5 * (vnl + vnr)
    half_t = 0.5 * (vtl + vtr)
    mass = mean * half_n
    if scale != 1.0:
        mass = mass * scale
    normal = mass * half_n + (0.5 * scale) * (fl[2] + fr[2])
    along = mass * half_t
    energy = mass * (0.5 * (vnl * vnr + vtl * vtr) + thermal) + (0.5 * scale) * (
        fl[2] * vnr + fr[2] * vnl
    )
    return (mass, normal, along, energy) if axis == 0 else (mass, along, normal, energy)


def face_flux(left, right, axis):
    (ul, fl), (ur, fr) = left, right
    centre = two_point(left, right, axis, 1.0)
    speed = 0.5 * jnp.maximum(jnp.abs(fl[axis]) + fl[6], jnp.abs(fr[axis]) + fr[6])
    return [centre[v] - speed * (ur[v] - ul[v]) for v in range(VARS)]


def physical(node, axis):
    u, f = node
    vn = f[axis]
    flux = [u[0] * vn, u[1] * vn, u[2] * vn, (u[3] + f[2]) * vn]
    flux[0] = u[1 + axis]
    flux[1 + axis] = flux[1 + axis] + f[2]
    return flux


def line_fluxes(nodes, axis, blend):
    pair = {}
    for a in range(4):
        for b in range(a + 1, 4):
            weight = float(2.0 * WEIGHTS[a] * DERIVATIVE[a, b])
            pair[a, b] = two_point(nodes[a], nodes[b], axis, weight)
    phys = [physical(node, axis) for node in nodes]
    fast = [jnp.abs(node[1][axis]) + node[1][6] for node in nodes]
    speeds = [jnp.maximum(fast[k], fast[k + 1]) for k in range(3)]
    result = [[], [], []]
    for v in range(VARS):
        far = pair[0, 3][v]
        head = pair[0, 2][v] + far
        tail = pair[1, 3][v]
        high = [pair[0, 1][v] + head, head + (pair[1, 2][v] + tail), (far + tail) + pair[2, 3][v]]
        for k in range(3):
            low = 0.5 * (
                (phys[k][v] + phys[k + 1][v])
                - speeds[k] * (nodes[k + 1][0][v] - nodes[k][0][v])
            )
            result[k].append(high[k] + blend * (low - high[k]))
    return result


def rolled(node, shift, axis):
    return tuple(tuple(pltpu.roll(x, shift, axis) for x in part) for part in node)


def coarse(u, factor):
    mean = None
    for i in range(4):
        for j in range(4):
            term = QUAD[i][j] * u[i][j]
            mean = term if mean is None else mean + term
    return [[mean + factor * (u[i][j] - mean) for j in range(4)] for i in range(4)]


def kernel(
    n_space,
    n_tm,
    o_hbm,
    fac_hbm,
    bw_hbm,
    bf_hbm,
    end_ref,
    norm_ref,
    o_ref,
    fac_ref,
    bw_ref,
    bf_ref,
    u_ref,
    w_ref,
    fld,
    acc,
    blend_ref,
    low_ref,
    high_ref,
    from_left,
    from_right,
    edge_ref,
    corr,
    mate,
    pairs,
    start_ref,
    jump_ref,
    halo_send,
    halo_recv,
    corr_send,
    corr_recv,
    chain_send,
    chain_recv,
    fwd_send,
    fwd_recv,
    jump_send,
    jump_recv,
    load_sem,
):
    rows, lanes = bw_ref.shape
    loads = [
        pltpu.make_async_copy(src, dst, load_sem.at[k])
        for k, (src, dst) in enumerate(
            ((o_hbm, o_ref), (fac_hbm, fac_ref), (bw_hbm, bw_ref), (bf_hbm, bf_ref))
        )
    ]
    for copy in loads:
        copy.start()
    sp = lax.axis_index("space")
    tm = lax.axis_index("tm")
    core = lax.rem(tm, 2)
    z = lax.div(tm, 2)
    partner = tm + 1 - 2 * core
    chips = n_tm // 2
    left = lax.rem(sp + n_space - 1, n_space)
    right = lax.rem(sp + 1, n_space)
    takes = jnp.logical_and(core == 1, z > 0)
    gives = jnp.logical_and(core == 1, z < chips - 1)

    barrier = pltpu.get_barrier_semaphore()
    for k in range(1, n_space):
        other = lax.rem(sp + k, n_space)
        pl.semaphore_signal(barrier, inc=1, device_id={"space": other}, device_id_type=MESH)
    pl.semaphore_signal(barrier, inc=1, device_id={"tm": partner}, device_id_type=MESH)

    @pl.when(takes)
    def _():
        pl.semaphore_signal(barrier, inc=1, device_id={"tm": tm - 2}, device_id_type=MESH)

    @pl.when(gives)
    def _():
        pl.semaphore_signal(barrier, inc=1, device_id={"tm": tm + 2}, device_id_type=MESH)

    for copy in loads:
        copy.wait()
    blend_ref[...] = bf_ref[...].astype(jnp.float32) * bw_ref[...]
    for v in range(VARS):
        for j in range(4):
            low = o_ref[0, v, 0, j, 0:1, :]
            high = o_ref[0, v, 3, j, rows - 1 : rows, :]
            for base in (0, 4):
                low_ref[0, v, base + j : base + j + 1, :] = low
                high_ref[0, v, base + j : base + j + 1, :] = high
    u_ref[...] = o_ref[0]

    peers = n_space + takes.astype(jnp.int32) + gives.astype(jnp.int32)
    pl.semaphore_wait(barrier, peers)

    def halo(slot):
        return (
            pltpu.make_async_remote_copy(
                src_ref=low_ref.at[slot],
                dst_ref=from_right.at[slot],
                send_sem=halo_send.at[slot, 0],
                recv_sem=halo_recv.at[slot, 0],
                device_id={"space": left},
                device_id_type=MESH,
            ),
            pltpu.make_async_remote_copy(
                src_ref=high_ref.at[slot],
                dst_ref=from_left.at[slot],
                send_sem=halo_send.at[slot, 1],
                recv_sem=halo_recv.at[slot, 1],
                device_id={"space": right},
                device_id_type=MESH,
            ),
        )

    for copy in halo(0):
        copy.start()

    row_at = lax.broadcasted_iota(jnp.int32, (rows, lanes), 0)
    first_row = row_at == 0
    last_row = row_at == rows - 1
    upper_half = lax.broadcasted_iota(jnp.int32, (8, lanes), 0) < 4
    gain = [float(-2.0 / WEIGHTS[i]) for i in range(4)]

    def stage(slot, src, dst, keep, more):
        fresh = 1.0 - keep
        fresh_step = fresh * step_size

        def load(i, j):
            u = tuple(src[v, i, j] for v in range(VARS))
            return (u, tuple(fld[k, i, j] for k in range(7)))

        for i in range(4):
            for j in range(4):
                values = node_fields(tuple(src[v, i, j] for v in range(VARS)))
                for k in range(7):
                    fld[k, i, j] = values[k]
        blend = blend_ref[...]

        def across(t):
            nodes = [load(i, t) for i in range(4)]
            inner = line_fluxes(nodes, 0, blend)
            face = face_flux(rolled(nodes[3], 1, 0), nodes[0], 0)
            for v in range(VARS):
                lower = jnp.where(first_row, 0.0, face[v])
                upper = jnp.where(last_row, 0.0, pltpu.roll(face[v], rows - 1, 0))
                walls = [lower, inner[0][v], inner[1][v], inner[2][v], upper]
                for i in range(4):
                    acc[v, i, t] = gain[i] * (walls[i + 1] - walls[i])

        def upward(t):
            nodes = [load(t, j) for j in range(4)]
            inner = line_fluxes(nodes, 1, blend)
            face = face_flux(rolled(nodes[3], 1, 1), nodes[0], 1)
            for v in range(VARS):
                upper = pltpu.roll(face[v], lanes - 1, 1)
                walls = [face[v], inner[0][v], inner[1][v], inner[2][v], upper]
                for j in range(4):
                    total = acc[v, t, j] + gain[j] * (walls[j + 1] - walls[j])
                    value = fresh * nodes[j][0][v] + fresh_step * total
                    if keep:
                        value = value + keep * dst[v, t, j]
                    dst[v, t, j] = value

        for t in range(4):
            across(t)
        for t in (1, 2):
            upward(t)

        for copy in halo(slot):
            copy.wait()

        uleft = tuple(
            jnp.where(upper_half, from_left[slot, v], high_ref[slot, v]) for v in range(VARS)
        )
        uright = tuple(
            jnp.where(upper_half, low_ref[slot, v], from_right[slot, v]) for v in range(VARS)
        )
        edge = face_flux((uleft, node_fields(uleft)), (uright, node_fields(uright)), 0)
        factor = jnp.where(upper_half, -gain[0] * fresh_step, gain[3] * fresh_step)
        for v in range(VARS):
            edge_ref[v] = factor * edge[v]
        for t in (0, 3):
            upward(t)
        other = 1 - slot
        for v in range(VARS):
            for j in range(4):
                low = dst[v, 0, j, 0:1, :] + edge_ref[v, j : j + 1, :]
                high = dst[v, 3, j, rows - 1 : rows, :] + edge_ref[v, 4 + j : 5 + j, :]
                dst[v, 0, j, 0:1, :] = low
                dst[v, 3, j, rows - 1 : rows, :] = high
                for base in (0, 4):
                    low_ref[other, v, base + j : base + j + 1, :] = low
                    high_ref[other, v, base + j : base + j + 1, :] = high

        @pl.when(more)
        def _():
            for copy in halo(other):
                copy.start()

    def fine_step(step, _):
        stage(0, u_ref, w_ref, 0.0, step < FSTEPS)
        stage(1, w_ref, u_ref, 0.5, step < FSTEPS - 1)
        return 0

    lax.fori_loop(0, FSTEPS, fine_step, 0)

    def grid_of(view):
        return [[view(i, j) for j in range(4)] for i in range(4)]

    def pass_on(src, dst, send, recv, v, device):
        return pltpu.make_async_remote_copy(
            src_ref=src.at[v],
            dst_ref=dst.at[v],
            send_sem=send.at[v],
            recv_sem=recv.at[v],
            device_id={"tm": device},
            device_id_type=MESH,
        )

    def to_mate(v):
        return pass_on(corr, mate, corr_send, corr_recv, v, partner)

    def to_next(v):
        return pass_on(end_ref.at[0], start_ref, chain_send, chain_recv, v, tm + 2)

    def to_first(v):
        return pass_on(start_ref, start_ref, fwd_send, fwd_recv, v, partner)

    counted = jnp.where(tm == 0, 0.0, 1.0)
    for v in range(VARS):
        base = coarse(grid_of(lambda i, j: o_ref[0, v, i, j]), fac_ref[v])
        for i in range(4):
            for j in range(4):
                corr[v, i, j] = u_ref[v, i, j] - counted * base[i][j]

        @pl.when(core == 0)
        def _():
            to_mate(v).start()

    jump_ref[0] = jnp.zeros((rows, lanes), jnp.float32)

    @pl.when(core == 0)
    def _():
        @pl.when(z == 0)
        def _():
            end_ref[0] = corr[...]

        @pl.when(z > 0)
        def _():
            total = jnp.zeros((rows, lanes), jnp.float32)
            for v in range(VARS):
                to_first(v).wait_recv()
                begun = grid_of(lambda i, j: start_ref[v, i, j])
                ended = coarse(begun, fac_ref[v])
                for i in range(4):
                    for j in range(4):
                        jump = begun[i][j] - o_ref[0, v, i, j]
                        total = total + QUAD[i][j] * (jump * jump)
                        end_ref[0, v, i, j] = ended[i][j] + corr[v, i, j]
            jump_ref[0] = total

        for v in range(VARS):
            to_mate(v).wait_send()

    @pl.when(core == 1)
    def _():
        @pl.when(z == 0)
        def _():
            start_ref[...] = jnp.zeros_like(start_ref)

        for v in range(VARS):
            to_mate(v).wait_recv()
            half = coarse(grid_of(lambda i, j: mate[v, i, j]), fac_ref[v])
            for i in range(4):
                for j in range(4):
                    pairs[v, i, j] = half[i][j] + corr[v, i, j]

        for v in range(VARS):

            @pl.when(z > 0)
            def _():
                to_next(v).wait_recv()
                to_first(v).start()

            factor = fac_ref[v]
            ended = coarse(grid_of(lambda i, j: start_ref[v, i, j]), factor * factor)
            for i in range(4):
                for j in range(4):
                    end_ref[0, v, i, j] = ended[i][j] + pairs[v, i, j]

            @pl.when(gives)
            def _():
                to_next(v).start()

        total = jnp.zeros((rows, lanes), jnp.float32)
        for v in range(VARS):
            begun = coarse(grid_of(lambda i, j: start_ref[v, i, j]), fac_ref[v])
            for i in range(4):
                for j in range(4):
                    jump = (begun[i][j] + mate[v, i, j]) - o_ref[0, v, i, j]
                    total = total + QUAD[i][j] * (jump * jump)
        jump_ref[0] = total

    def share(k):
        return pltpu.make_async_remote_copy(
            src_ref=jump_ref.at[0],
            dst_ref=jump_ref.at[k],
            send_sem=jump_send.at[k],
            recv_sem=jump_recv.at[k],
            device_id={"space": lax.rem(sp + k, n_space)},
            device_id_type=MESH,
        )

    for k in range(1, n_space):
        share(k).start()

    @pl.when(takes)
    def _():
        for v in range(VARS):
            to_first(v).wait_send()

    @pl.when(gives)
    def _():
        for v in range(VARS):
            to_next(v).wait_send()

    for k in range(1, n_space):
        share(k).wait()
    total = jump_ref[0]
    for k in range(1, n_space):
        total = total + jump_ref[k]
    total = jnp.sum(jnp.sum(total, axis=0, keepdims=True), axis=1, keepdims=True)
    norm_ref[...] = jnp.broadcast_to(
        jnp.sqrt(total * (1.0 / (n_space * rows * lanes))), norm_ref.shape
    )


def solution(mesh):
    n_tm = mesh.shape["tm"]
    n_space = mesh.shape["space"]

    def on_device(slab_starts, coarse_factor, blend_weight, blend_flags):
        rows, lanes = blend_weight.shape
        state = (VARS, NODES, NODES, rows, lanes)
        f32 = jnp.float32
        dma = pltpu.SemaphoreType.DMA
        vmem = pl.BlockSpec(memory_space=pltpu.VMEM)
        edges = pltpu.VMEM((2, VARS, 8, lanes), f32)
        ends, norm = pl.pallas_call(
            functools.partial(kernel, n_space, n_tm),
            out_shape=(
                jax.ShapeDtypeStruct((1,) + state, f32),
                jax.ShapeDtypeStruct((1, 128), f32),
            ),
            in_specs=[pl.BlockSpec(memory_space=pltpu.HBM)] * 4,
            out_specs=(vmem, vmem),
            scratch_shapes=[
                pltpu.VMEM((1,) + state, f32),
                pltpu.VMEM(coarse_factor.shape, f32),
                pltpu.VMEM(blend_weight.shape, f32),
                pltpu.VMEM(blend_flags.shape, blend_flags.dtype),
                pltpu.VMEM(state, f32),
                pltpu.VMEM(state, f32),
                pltpu.VMEM((7, NODES, NODES, rows, lanes), f32),
                pltpu.VMEM(state, f32),
                pltpu.VMEM((rows, lanes), f32),
                edges,
                edges,
                edges,
                edges,
                pltpu.VMEM((VARS, 8, lanes), f32),
                pltpu.VMEM(state, f32),
                pltpu.VMEM(state, f32),
                pltpu.VMEM(state, f32),
                pltpu.VMEM(state, f32),
                pltpu.VMEM((n_space, rows, lanes), f32),
                dma((2, 2)),
                dma((2, 2)),
                dma((VARS,)),
                dma((VARS,)),
                dma((VARS,)),
                dma((VARS,)),
                dma((VARS,)),
                dma((VARS,)),
                dma((n_space,)),
                dma((n_space,)),
                dma((4,)),
            ],
            compiler_params=pltpu.CompilerParams(
                collective_id=0, has_side_effects=True, vmem_limit_bytes=32 * 1024 * 1024
            ),
        )(slab_starts, coarse_factor, blend_weight, blend_flags)
        return ends, norm[0, :1]

    in_specs = (
        P("tm", None, None, None, "space", None),
        P(None, "space", None),
        P("space", None),
        P("space", None),
    )
    out_specs = (P("tm", None, None, None, "space", None), P("tm"))
    return jax.shard_map(
        on_device, mesh=mesh, in_specs=in_specs, out_specs=out_specs, check_vma=False
    )
```

```python
import functools
import math

import jax
import jax.numpy as jnp
import numpy as np
from jax import lax
from jax.experimental import pallas as pl
from jax.experimental.pallas import tpu as pltpu
from jax.sharding import PartitionSpec as P

FSTEPS = 4
NODES = 4
VARS = 4

gamma_ratio = 1.4
step_size = 0.003
MESH = pl.DeviceIdType.MESH


def tables():
    inner = 1.0 / math.sqrt(5.0)
    points = np.array([-1.0, -inner, inner, 1.0])
    weights = np.array([1.0 / 6.0, 5.0 / 6.0, 5.0 / 6.0, 1.0 / 6.0])
    scales = [
        1.0 / np.prod([points[c] - points[k] for k in range(4) if k != c]) for c in range(4)
    ]
    derivative = np.zeros((4, 4))
    for r in range(4):
        for c in range(4):
            if r != c:
                derivative[r, c] = scales[c] / scales[r] / (points[r] - points[c])
    return derivative, weights


DERIVATIVE, WEIGHTS = tables()
QUAD = [[float(WEIGHTS[i] * WEIGHTS[j] / 4.0) for j in range(4)] for i in range(4)]


def rough(x):
    return pl.reciprocal(x, approx=True)


def inverse(x):
    r = pl.reciprocal(x, approx=True)
    return r * (2.0 - x * r)


def near_terms(a, b):
    total = a + b
    differ = b - a
    ratio = differ * rough(total)
    ratio = ratio * ratio
    series = 2.0 + ratio * (35.0 / 52.5 + ratio * (21.0 / 52.5 + ratio * (15.0 / 52.5)))
    return ratio < 0.0001, total, differ, series


def node_fields(u):
    rho, mx, my, energy = u
    ir = inverse(rho)
    vx = mx * ir
    vy = my * ir
    p = 0.4 * energy - 0.2 * (mx * vx + my * vy)
    beta = rho * inverse(p)
    warm = gamma_ratio * p * ir
    sound = warm * lax.rsqrt(warm)
    return (vx, vy, p, beta, jnp.log(rho), 2.5 * jnp.log(beta), sound)


def two_point(left, right, axis, scale):
    (ul, fl), (ur, fr) = left, right
    vnl, vtl = (fl[0], fl[1]) if axis == 0 else (fl[1], fl[0])
    vnr, vtr = (fr[0], fr[1]) if axis == 0 else (fr[1], fr[0])
    near, total, differ, series = near_terms(ul[0], ur[0])
    mean = jnp.where(near, total, differ) * inverse(jnp.where(near, series, fr[4] - fl[4]))
    near, total, differ, series = near_terms(fl[3], fr[3])
    thermal = jnp.where(near, 2.5 * series, fr[5] - fl[5]) * inverse(
        jnp.where(near, total, differ)
    )
    half_n = 0.5 * (vnl + vnr)
    half_t = 0.5 * (vtl + vtr)
    mass = mean * half_n
    if scale != 1.0:
        mass = mass * scale
    normal = mass * half_n + (0.5 * scale) * (fl[2] + fr[2])
    along = mass * half_t
    energy = mass * (0.5 * (vnl * vnr + vtl * vtr) + thermal) + (0.5 * scale) * (
        fl[2] * vnr + fr[2] * vnl
    )
    return (mass, normal, along, energy) if axis == 0 else (mass, along, normal, energy)


def face_flux(left, right, axis):
    (ul, fl), (ur, fr) = left, right
    centre = two_point(left, right, axis, 1.0)
    speed = 0.5 * jnp.maximum(jnp.abs(fl[axis]) + fl[6], jnp.abs(fr[axis]) + fr[6])
    return [centre[v] - speed * (ur[v] - ul[v]) for v in range(VARS)]


def physical(node, axis):
    u, f = node
    vn = f[axis]
    flux = [u[0] * vn, u[1] * vn, u[2] * vn, (u[3] + f[2]) * vn]
    flux[0] = u[1 + axis]
    flux[1 + axis] = flux[1 + axis] + f[2]
    return flux


def line_fluxes(nodes, axis, blend):
    pair = {}
    for a in range(4):
        for b in range(a + 1, 4):
            weight = float(2.0 * WEIGHTS[a] * DERIVATIVE[a, b])
            pair[a, b] = two_point(nodes[a], nodes[b], axis, weight)
    phys = [physical(node, axis) for node in nodes]
    fast = [jnp.abs(node[1][axis]) + node[1][6] for node in nodes]
    speeds = [jnp.maximum(fast[k], fast[k + 1]) for k in range(3)]
    result = [[], [], []]
    for v in range(VARS):
        far = pair[0, 3][v]
        head = pair[0, 2][v] + far
        tail = pair[1, 3][v]
        high = [pair[0, 1][v] + head, head + (pair[1, 2][v] + tail), (far + tail) + pair[2, 3][v]]
        for k in range(3):
            low = 0.5 * (
                (phys[k][v] + phys[k + 1][v])
                - speeds[k] * (nodes[k + 1][0][v] - nodes[k][0][v])
            )
            result[k].append(high[k] + blend * (low - high[k]))
    return result


def rolled(node, shift, axis):
    return tuple(tuple(pltpu.roll(x, shift, axis) for x in part) for part in node)


def coarse(u, factor):
    mean = None
    for i in range(4):
        for j in range(4):
            term = QUAD[i][j] * u[i][j]
            mean = term if mean is None else mean + term
    return [[mean + factor * (u[i][j] - mean) for j in range(4)] for i in range(4)]


def kernel(
    n_space,
    n_tm,
    o_hbm,
    fac_hbm,
    bw_hbm,
    bf_hbm,
    end_ref,
    norm_ref,
    o_ref,
    fac_ref,
    bw_ref,
    bf_ref,
    u_ref,
    w_ref,
    fld,
    acc,
    blend_ref,
    low_ref,
    high_ref,
    from_left,
    from_right,
    edge_ref,
    own_ref,
    near_ref,
    corr,
    mate,
    pairs,
    start_ref,
    jump_ref,
    halo_send,
    halo_recv,
    corr_send,
    corr_recv,
    chain_send,
    chain_recv,
    fwd_send,
    fwd_recv,
    jump_send,
    jump_recv,
    load_sem,
):
    rows, lanes = bw_ref.shape
    loads = [
        pltpu.make_async_copy(src, dst, load_sem.at[k])
        for k, (src, dst) in enumerate(
            ((o_hbm, o_ref), (fac_hbm, fac_ref), (bw_hbm, bw_ref), (bf_hbm, bf_ref))
        )
    ]
    for copy in loads:
        copy.start()
    sp = lax.axis_index("space")
    tm = lax.axis_index("tm")
    core = lax.rem(tm, 2)
    z = lax.div(tm, 2)
    partner = tm + 1 - 2 * core
    chips = n_tm // 2
    left = lax.rem(sp + n_space - 1, n_space)
    right = lax.rem(sp + 1, n_space)
    takes = jnp.logical_and(core == 1, z > 0)
    gives = jnp.logical_and(core == 1, z < chips - 1)

    barrier = pltpu.get_barrier_semaphore()
    for k in range(1, n_space):
        other = lax.rem(sp + k, n_space)
        pl.semaphore_signal(barrier, inc=1, device_id={"space": other}, device_id_type=MESH)
    pl.semaphore_signal(barrier, inc=1, device_id={"tm": partner}, device_id_type=MESH)

    @pl.when(takes)
    def _():
        pl.semaphore_signal(barrier, inc=1, device_id={"tm": tm - 2}, device_id_type=MESH)

    @pl.when(gives)
    def _():
        pl.semaphore_signal(barrier, inc=1, device_id={"tm": tm + 2}, device_id_type=MESH)

    for copy in loads:
        copy.wait()
    blend_ref[...] = bf_ref[...].astype(jnp.float32) * bw_ref[...]
    for slot in range(2):
        low_ref[slot, 2 * VARS] = jnp.broadcast_to(blend_ref[0:1, :], (8, lanes))
        high_ref[slot, 2 * VARS] = jnp.broadcast_to(blend_ref[rows - 1 : rows, :], (8, lanes))

    def pack(slot):
        for v in range(VARS):
            for d in range(4):
                for j in range(4):
                    at = 4 * (d % 2) + j
                    low_ref[slot, 2 * v + d // 2, at : at + 1, :] = u_ref[v, d, j, 0:1, :]
                    high_ref[slot, 2 * v + d // 2, at : at + 1, :] = u_ref[
                        v, 3 - d, j, rows - 1 : rows, :
                    ]

    u_ref[...] = o_ref[0]
    pack(0)

    peers = n_space + takes.astype(jnp.int32) + gives.astype(jnp.int32)
    pl.semaphore_wait(barrier, peers)

    def halo(slot):
        return (
            pltpu.make_async_remote_copy(
                src_ref=low_ref.at[slot],
                dst_ref=from_right.at[slot],
                send_sem=halo_send.at[slot, 0],
                recv_sem=halo_recv.at[slot, 0],
                device_id={"space": left},
                device_id_type=MESH,
            ),
            pltpu.make_async_remote_copy(
                src_ref=high_ref.at[slot],
                dst_ref=from_left.at[slot],
                send_sem=halo_send.at[slot, 1],
                recv_sem=halo_recv.at[slot, 1],
                device_id={"space": right},
                device_id_type=MESH,
            ),
        )

    for copy in halo(0):
        copy.start()

    row_at = lax.broadcasted_iota(jnp.int32, (rows, lanes), 0)
    first_row = row_at == 0
    last_row = row_at == rows - 1
    upper_half = lax.broadcasted_iota(jnp.int32, (8, lanes), 0) < 4
    gain = [float(-2.0 / WEIGHTS[i]) for i in range(4)]

    sub = lax.rem(lax.broadcasted_iota(jnp.int32, (8, lanes), 0), 4)

    def by_node(values):
        return jnp.where(
            sub == 0, values[0], jnp.where(sub == 1, values[1], jnp.where(sub == 2, values[2], values[3]))
        )

    def choose(mask, left, right):
        return tuple(
            tuple(jnp.where(mask, a, b) for a, b in zip(p, q)) for p, q in zip(left, right)
        )

    def lane_rolled(node, shift):
        return rolled(node, shift, 1)

    def coefficient(a, b):
        return float(2.0 * WEIGHTS[a] * DERIVATIVE[a, b])

    side = jnp.where(upper_half, 1.0, -1.0)

    def outside(nodes, edge, blend):
        near = nodes[0]
        high = [0.0] * VARS
        for d in (1, 2, 3):
            term = two_point(nodes[d], near, 0, coefficient(3 - d, 3))
            high = [high[v] + term[v] for v in range(VARS)]
        phys = [physical(nodes[d], 0) for d in (0, 1)]
        fast = [jnp.abs(nodes[d][1][0]) + nodes[d][1][6] for d in (0, 1)]
        speed = side * jnp.maximum(fast[0], fast[1])
        rate = []
        for v in range(VARS):
            low = 0.5 * (phys[0][v] + phys[1][v] - speed * (near[0][v] - nodes[1][0][v]))
            inner = high[v] + blend * (low - high[v])
            rate.append((gain[3] * side) * (edge[v] - inner))

        wrapped = rolled(near, 5, 0)
        before = choose(sub == 0, lane_rolled(wrapped, 1), rolled(near, 1, 0))
        first = two_point(before, near, 1, 1.0)
        second = two_point(choose(sub == 0, wrapped, rolled(near, 2, 0)), near, 1, 1.0)
        first_scale = by_node([0.0, coefficient(0, 1), coefficient(1, 2), coefficient(2, 3)])
        second_scale = by_node([coefficient(0, 3), 0.0, coefficient(0, 2), coefficient(1, 3)])
        before_phys, near_phys = physical(before, 1), physical(near, 1)
        speed = 0.5 * jnp.maximum(
            jnp.abs(before[1][1]) + before[1][6], jnp.abs(near[1][1]) + near[1][6]
        )
        gains = by_node(gain)
        result = []
        for v in range(VARS):
            damping = speed * (near[0][v] - before[0][v])
            far = second_scale * second[v]
            high = first_scale * first[v] + jnp.where(sub >= 2, far, 0.0)
            high = high + jnp.where(
                jnp.logical_or(sub == 1, sub == 2), pltpu.roll(far, 7, 0), 0.0
            )
            high = high + by_node(
                [0.0, pltpu.roll(far, 1, 0), pltpu.roll(far, 2, 0), pltpu.roll(far, 3, 0)]
            )
            low = 0.5 * (before_phys[v] + near_phys[v]) - damping
            wall = jnp.where(sub == 0, first[v] - damping, high + blend * (low - high))
            above = jnp.where(
                sub == 3,
                pltpu.roll(pltpu.roll(wall, 3, 0), lanes - 1, 1),
                pltpu.roll(wall, 7, 0),
            )
            result.append(near[0][v] + step_size * (rate[v] + gains * (above - wall)))
        return result

    def stage(first, slot, src, dst, keep):
        fresh = 1.0 - keep
        fresh_step = fresh * step_size

        def load(i, j):
            u = tuple(src[v, i, j] for v in range(VARS))
            return (u, tuple(fld[k, i, j] for k in range(7)))

        for i in range(4):
            for j in range(4):
                values = node_fields(tuple(src[v, i, j] for v in range(VARS)))
                for k in range(7):
                    fld[k, i, j] = values[k]
        blend = blend_ref[...]

        def across(t):
            nodes = [load(i, t) for i in range(4)]
            inner = line_fluxes(nodes, 0, blend)
            face = face_flux(rolled(nodes[3], 1, 0), nodes[0], 0)
            for v in range(VARS):
                lower = jnp.where(first_row, 0.0, face[v])
                upper = jnp.where(last_row, 0.0, pltpu.roll(face[v], rows - 1, 0))
                walls = [lower, inner[0][v], inner[1][v], inner[2][v], upper]
                for i in range(4):
                    acc[v, i, t] = gain[i] * (walls[i + 1] - walls[i])

        def upward(t):
            nodes = [load(t, j) for j in range(4)]
            inner = line_fluxes(nodes, 1, blend)
            face = face_flux(rolled(nodes[3], 1, 1), nodes[0], 1)
            for v in range(VARS):
                upper = pltpu.roll(face[v], lanes - 1, 1)
                walls = [face[v], inner[0][v], inner[1][v], inner[2][v], upper]
                for j in range(4):
                    total = acc[v, t, j] + gain[j] * (walls[j + 1] - walls[j])
                    value = fresh * nodes[j][0][v] + fresh_step * total
                    if keep:
                        value = value + keep * dst[v, t, j]
                    dst[v, t, j] = value

        for t in range(4):
            across(t)
        for t in (1, 2):
            upward(t)

        if first:
            for copy in halo(slot):
                copy.wait()

            def packed(v, d):
                left_tile = from_left[slot, 2 * v + d // 2]
                right_tile = from_right[slot, 2 * v + d // 2]
                if d % 2:
                    left_tile = pltpu.roll(left_tile, 4, 0)
                else:
                    right_tile = pltpu.roll(right_tile, 4, 0)
                return jnp.where(upper_half, left_tile, right_tile)

            values = [tuple(packed(v, d) for v in range(VARS)) for d in range(4)]
            beyond = [(u, node_fields(u)) for u in values]
            own = tuple(
                jnp.where(upper_half, low_ref[slot, 2 * v], pltpu.roll(high_ref[slot, 2 * v], 4, 0))
                for v in range(VARS)
            )
        else:
            u = tuple(near_ref[v] for v in range(VARS))
            beyond = [(u, node_fields(u))]
            own = tuple(own_ref[v] for v in range(VARS))
        own = (own, node_fields(own))
        edge = face_flux(
            choose(upper_half, beyond[0], own), choose(upper_half, own, beyond[0]), 0
        )
        factor = jnp.where(upper_half, -gain[0] * fresh_step, gain[3] * fresh_step)
        for v in range(VARS):
            edge_ref[v] = factor * edge[v]
        if first:
            outer_blend = jnp.where(
                upper_half, from_left[slot, 2 * VARS], from_right[slot, 2 * VARS]
            )
            stepped = outside(beyond, edge, outer_blend)
            for v in range(VARS):
                near_ref[v] = stepped[v]
        for t in (0, 3):
            upward(t)
        for v in range(VARS):
            for j in range(4):
                low = dst[v, 0, j, 0:1, :] + edge_ref[v, j : j + 1, :]
                high = dst[v, 3, j, rows - 1 : rows, :] + edge_ref[v, 4 + j : 5 + j, :]
                dst[v, 0, j, 0:1, :] = low
                dst[v, 3, j, rows - 1 : rows, :] = high
                if first:
                    own_ref[v, j : j + 1, :] = low
                    own_ref[v, 4 + j : 5 + j, :] = high

    def fine_step(step, _):
        slot = lax.rem(step, 2)
        stage(True, slot, u_ref, w_ref, 0.0)
        stage(False, slot, w_ref, u_ref, 0.5)

        @pl.when(step < FSTEPS - 1)
        def _():
            pack(1 - slot)
            for copy in halo(1 - slot):
                copy.start()

        return 0

    lax.fori_loop(0, FSTEPS, fine_step, 0)

    def grid_of(view):
        return [[view(i, j) for j in range(4)] for i in range(4)]

    def pass_on(src, dst, send, recv, v, device):
        return pltpu.make_async_remote_copy(
            src_ref=src.at[v],
            dst_ref=dst.at[v],
            send_sem=send.at[v],
            recv_sem=recv.at[v],
            device_id={"tm": device},
            device_id_type=MESH,
        )

    def to_mate(v):
        return pass_on(corr, mate, corr_send, corr_recv, v, partner)

    def to_next(v):
        return pass_on(end_ref.at[0], start_ref, chain_send, chain_recv, v, tm + 2)

    def to_first(v):
        return pass_on(start_ref, start_ref, fwd_send, fwd_recv, v, partner)

    counted = jnp.where(tm == 0, 0.0, 1.0)
    for v in range(VARS):
        base = coarse(grid_of(lambda i, j: o_ref[0, v, i, j]), fac_ref[v])
        for i in range(4):
            for j in range(4):
                corr[v, i, j] = u_ref[v, i, j] - counted * base[i][j]

        @pl.when(core == 0)
        def _():
            to_mate(v).start()

    jump_ref[0] = jnp.zeros((rows, lanes), jnp.float32)

    @pl.when(core == 0)
    def _():
        @pl.when(z == 0)
        def _():
            end_ref[0] = corr[...]

        @pl.when(z > 0)
        def _():
            total = jnp.zeros((rows, lanes), jnp.float32)
            for v in range(VARS):
                to_first(v).wait_recv()
                begun = grid_of(lambda i, j: start_ref[v, i, j])
                ended = coarse(begun, fac_ref[v])
                for i in range(4):
                    for j in range(4):
                        jump = begun[i][j] - o_ref[0, v, i, j]
                        total = total + QUAD[i][j] * (jump * jump)
                        end_ref[0, v, i, j] = ended[i][j] + corr[v, i, j]
            jump_ref[0] = total

        for v in range(VARS):
            to_mate(v).wait_send()

    @pl.when(core == 1)
    def _():
        @pl.when(z == 0)
        def _():
            start_ref[...] = jnp.zeros_like(start_ref)

        for v in range(VARS):
            to_mate(v).wait_recv()
            half = coarse(grid_of(lambda i, j: mate[v, i, j]), fac_ref[v])
            for i in range(4):
                for j in range(4):
                    pairs[v, i, j] = half[i][j] + corr[v, i, j]

        for v in range(VARS):

            @pl.when(z > 0)
            def _():
                to_next(v).wait_recv()
                to_first(v).start()

            factor = fac_ref[v]
            ended = coarse(grid_of(lambda i, j: start_ref[v, i, j]), factor * factor)
            for i in range(4):
                for j in range(4):
                    end_ref[0, v, i, j] = ended[i][j] + pairs[v, i, j]

            @pl.when(gives)
            def _():
                to_next(v).start()

        total = jnp.zeros((rows, lanes), jnp.float32)
        for v in range(VARS):
            begun = coarse(grid_of(lambda i, j: start_ref[v, i, j]), fac_ref[v])
            for i in range(4):
                for j in range(4):
                    jump = (begun[i][j] + mate[v, i, j]) - o_ref[0, v, i, j]
                    total = total + QUAD[i][j] * (jump * jump)
        jump_ref[0] = total

    def share(k):
        return pltpu.make_async_remote_copy(
            src_ref=jump_ref.at[0],
            dst_ref=jump_ref.at[k],
            send_sem=jump_send.at[k],
            recv_sem=jump_recv.at[k],
            device_id={"space": lax.rem(sp + k, n_space)},
            device_id_type=MESH,
        )

    for k in range(1, n_space):
        share(k).start()

    @pl.when(takes)
    def _():
        for v in range(VARS):
            to_first(v).wait_send()

    @pl.when(gives)
    def _():
        for v in range(VARS):
            to_next(v).wait_send()

    for k in range(1, n_space):
        share(k).wait()
    total = jump_ref[0]
    for k in range(1, n_space):
        total = total + jump_ref[k]
    total = jnp.sum(jnp.sum(total, axis=0, keepdims=True), axis=1, keepdims=True)
    norm_ref[...] = jnp.broadcast_to(
        jnp.sqrt(total * (1.0 / (n_space * rows * lanes))), norm_ref.shape
    )


def solution(mesh):
    n_tm = mesh.shape["tm"]
    n_space = mesh.shape["space"]

    def on_device(slab_starts, coarse_factor, blend_weight, blend_flags):
        rows, lanes = blend_weight.shape
        state = (VARS, NODES, NODES, rows, lanes)
        f32 = jnp.float32
        dma = pltpu.SemaphoreType.DMA
        vmem = pl.BlockSpec(memory_space=pltpu.VMEM)
        edges = pltpu.VMEM((2, 2 * VARS + 1, 8, lanes), f32)
        ends, norm = pl.pallas_call(
            functools.partial(kernel, n_space, n_tm),
            out_shape=(
                jax.ShapeDtypeStruct((1,) + state, f32),
                jax.ShapeDtypeStruct((1, 128), f32),
            ),
            in_specs=[pl.BlockSpec(memory_space=pltpu.HBM)] * 4,
            out_specs=(vmem, vmem),
            scratch_shapes=[
                pltpu.VMEM((1,) + state, f32),
                pltpu.VMEM(coarse_factor.shape, f32),
                pltpu.VMEM(blend_weight.shape, f32),
                pltpu.VMEM(blend_flags.shape, blend_flags.dtype),
                pltpu.VMEM(state, f32),
                pltpu.VMEM(state, f32),
                pltpu.VMEM((7, NODES, NODES, rows, lanes), f32),
                pltpu.VMEM(state, f32),
                pltpu.VMEM((rows, lanes), f32),
                edges,
                edges,
                edges,
                edges,
                pltpu.VMEM((VARS, 8, lanes), f32),
                pltpu.VMEM((VARS, 8, lanes), f32),
                pltpu.VMEM((VARS, 8, lanes), f32),
                pltpu.VMEM(state, f32),
                pltpu.VMEM(state, f32),
                pltpu.VMEM(state, f32),
                pltpu.VMEM(state, f32),
                pltpu.VMEM((n_space, rows, lanes), f32),
                dma((2, 2)),
                dma((2, 2)),
                dma((VARS,)),
                dma((VARS,)),
                dma((VARS,)),
                dma((VARS,)),
                dma((VARS,)),
                dma((VARS,)),
                dma((n_space,)),
                dma((n_space,)),
                dma((4,)),
            ],
            compiler_params=pltpu.CompilerParams(
                collective_id=0, has_side_effects=True, vmem_limit_bytes=64 * 1024 * 1024
            ),
        )(slab_starts, coarse_factor, blend_weight, blend_flags)
        return ends, norm[0, :1]

    in_specs = (
        P("tm", None, None, None, "space", None),
        P(None, "space", None),
        P("space", None),
        P("space", None),
    )
    out_specs = (P("tm", None, None, None, "space", None), P("tm"))
    return jax.shard_map(
        on_device, mesh=mesh, in_specs=in_specs, out_specs=out_specs, check_vma=False
    )
```

```python
import functools
import math

import jax
import jax.numpy as jnp
import numpy as np
from jax import lax
from jax.experimental import pallas as pl
from jax.experimental.pallas import tpu as pltpu
from jax.sharding import PartitionSpec as P

FSTEPS = 4
NODES = 4
VARS = 4

gamma_ratio = 1.4
step_size = 0.003
MESH = pl.DeviceIdType.MESH


def tables():
    inner = 1.0 / math.sqrt(5.0)
    points = np.array([-1.0, -inner, inner, 1.0])
    weights = np.array([1.0 / 6.0, 5.0 / 6.0, 5.0 / 6.0, 1.0 / 6.0])
    scales = [
        1.0 / np.prod([points[c] - points[k] for k in range(4) if k != c]) for c in range(4)
    ]
    derivative = np.zeros((4, 4))
    for r in range(4):
        for c in range(4):
            if r != c:
                derivative[r, c] = scales[c] / scales[r] / (points[r] - points[c])
    return derivative, weights


DERIVATIVE, WEIGHTS = tables()
QUAD = [[float(WEIGHTS[i] * WEIGHTS[j] / 4.0) for j in range(4)] for i in range(4)]


def rough(x):
    return pl.reciprocal(x, approx=True)


def inverse(x):
    r = pl.reciprocal(x, approx=True)
    return r * (2.0 - x * r)


def near_terms(a, b):
    total = a + b
    differ = b - a
    ratio = differ * rough(total)
    ratio = ratio * ratio
    series = 2.0 + ratio * (35.0 / 52.5 + ratio * (21.0 / 52.5 + ratio * (15.0 / 52.5)))
    return ratio < 0.0001, total, differ, series


def node_fields(u):
    rho, mx, my, energy = u
    ir = inverse(rho)
    vx = mx * ir
    vy = my * ir
    p = 0.4 * energy - 0.2 * (mx * vx + my * vy)
    beta = rho * inverse(p)
    warm = gamma_ratio * p * ir
    sound = warm * lax.rsqrt(warm)
    return (vx, vy, p, beta, jnp.log(rho), 2.5 * jnp.log(beta), sound)


def two_point(left, right, axis, scale):
    (ul, fl), (ur, fr) = left, right
    vnl, vtl = (fl[0], fl[1]) if axis == 0 else (fl[1], fl[0])
    vnr, vtr = (fr[0], fr[1]) if axis == 0 else (fr[1], fr[0])
    near, total, differ, series = near_terms(ul[0], ur[0])
    mean = jnp.where(near, total, differ) * inverse(jnp.where(near, series, fr[4] - fl[4]))
    near, total, differ, series = near_terms(fl[3], fr[3])
    thermal = jnp.where(near, 2.5 * series, fr[5] - fl[5]) * inverse(
        jnp.where(near, total, differ)
    )
    half_n = 0.5 * (vnl + vnr)
    half_t = 0.5 * (vtl + vtr)
    mass = mean * half_n
    if scale != 1.0:
        mass = mass * scale
    normal = mass * half_n + (0.5 * scale) * (fl[2] + fr[2])
    along = mass * half_t
    energy = mass * (0.5 * (vnl * vnr + vtl * vtr) + thermal) + (0.5 * scale) * (
        fl[2] * vnr + fr[2] * vnl
    )
    return (mass, normal, along, energy) if axis == 0 else (mass, along, normal, energy)


def face_flux(left, right, axis):
    (ul, fl), (ur, fr) = left, right
    centre = two_point(left, right, axis, 1.0)
    speed = 0.5 * jnp.maximum(jnp.abs(fl[axis]) + fl[6], jnp.abs(fr[axis]) + fr[6])
    return [centre[v] - speed * (ur[v] - ul[v]) for v in range(VARS)]


def physical(node, axis):
    u, f = node
    vn = f[axis]
    flux = [u[0] * vn, u[1] * vn, u[2] * vn, (u[3] + f[2]) * vn]
    flux[0] = u[1 + axis]
    flux[1 + axis] = flux[1 + axis] + f[2]
    return flux


def line_fluxes(nodes, axis, blend):
    pair = {}
    for a in range(4):
        for b in range(a + 1, 4):
            weight = float(2.0 * WEIGHTS[a] * DERIVATIVE[a, b])
            pair[a, b] = two_point(nodes[a], nodes[b], axis, weight)
    phys = [physical(node, axis) for node in nodes]
    fast = [jnp.abs(node[1][axis]) + node[1][6] for node in nodes]
    speeds = [jnp.maximum(fast[k], fast[k + 1]) for k in range(3)]
    result = [[], [], []]
    for v in range(VARS):
        far = pair[0, 3][v]
        head = pair[0, 2][v] + far
        tail = pair[1, 3][v]
        high = [pair[0, 1][v] + head, head + (pair[1, 2][v] + tail), (far + tail) + pair[2, 3][v]]
        for k in range(3):
            low = 0.5 * (
                (phys[k][v] + phys[k + 1][v])
                - speeds[k] * (nodes[k + 1][0][v] - nodes[k][0][v])
            )
            result[k].append(high[k] + blend * (low - high[k]))
    return result


def rolled(node, shift, axis):
    return tuple(tuple(pltpu.roll(x, shift, axis) for x in part) for part in node)


def coarse(u, factor):
    mean = None
    for i in range(4):
        for j in range(4):
            term = QUAD[i][j] * u[i][j]
            mean = term if mean is None else mean + term
    return [[mean + factor * (u[i][j] - mean) for j in range(4)] for i in range(4)]


def kernel(
    n_space,
    n_tm,
    o_hbm,
    fac_hbm,
    bw_hbm,
    bf_hbm,
    end_hbm,
    norm_ref,
    end_ref,
    mean_in,
    mean_out,
    o_ref,
    fac_ref,
    bw_ref,
    bf_ref,
    u_ref,
    w_ref,
    fld,
    acc,
    blend_ref,
    low_ref,
    high_ref,
    from_left,
    from_right,
    edge_ref,
    own_ref,
    near_ref,
    corr,
    mate,
    pairs,
    start_ref,
    jump_ref,
    halo_send,
    halo_recv,
    corr_send,
    corr_recv,
    chain_send,
    chain_recv,
    fwd_send,
    fwd_recv,
    jump_send,
    jump_recv,
    load_sem,
    store_sem,
):
    rows, lanes = bw_ref.shape
    loads = [
        pltpu.make_async_copy(src, dst, load_sem.at[k])
        for k, (src, dst) in enumerate(
            ((o_hbm, o_ref), (fac_hbm, fac_ref), (bw_hbm, bw_ref), (bf_hbm, bf_ref))
        )
    ]
    for copy in loads:
        copy.start()
    sp = lax.axis_index("space")
    tm = lax.axis_index("tm")
    core = lax.rem(tm, 2)
    z = lax.div(tm, 2)
    partner = tm + 1 - 2 * core
    chips = n_tm // 2
    left = lax.rem(sp + n_space - 1, n_space)
    right = lax.rem(sp + 1, n_space)
    takes = jnp.logical_and(core == 1, z > 0)
    gives = jnp.logical_and(core == 1, z < chips - 1)

    barrier = pltpu.get_barrier_semaphore()
    for k in range(1, n_space):
        other = lax.rem(sp + k, n_space)
        pl.semaphore_signal(barrier, inc=1, device_id={"space": other}, device_id_type=MESH)
    pl.semaphore_signal(barrier, inc=1, device_id={"tm": partner}, device_id_type=MESH)

    @pl.when(takes)
    def _():
        pl.semaphore_signal(barrier, inc=1, device_id={"tm": tm - 2}, device_id_type=MESH)

    @pl.when(gives)
    def _():
        pl.semaphore_signal(barrier, inc=1, device_id={"tm": tm + 2}, device_id_type=MESH)

    for copy in loads:
        copy.wait()
    blend_ref[...] = bf_ref[...].astype(jnp.float32) * bw_ref[...]
    for slot in range(2):
        low_ref[slot, 2 * VARS] = jnp.broadcast_to(blend_ref[0:1, :], (8, lanes))
        high_ref[slot, 2 * VARS] = jnp.broadcast_to(blend_ref[rows - 1 : rows, :], (8, lanes))

    def pack(slot):
        for v in range(VARS):
            for d in range(4):
                for j in range(4):
                    at = 4 * (d % 2) + j
                    low_ref[slot, 2 * v + d // 2, at : at + 1, :] = u_ref[v, d, j, 0:1, :]
                    high_ref[slot, 2 * v + d // 2, at : at + 1, :] = u_ref[
                        v, 3 - d, j, rows - 1 : rows, :
                    ]

    u_ref[...] = o_ref[0]
    pack(0)

    peers = n_space + takes.astype(jnp.int32) + gives.astype(jnp.int32)
    pl.semaphore_wait(barrier, peers)

    def halo(slot):
        return (
            pltpu.make_async_remote_copy(
                src_ref=low_ref.at[slot],
                dst_ref=from_right.at[slot],
                send_sem=halo_send.at[slot, 0],
                recv_sem=halo_recv.at[slot, 0],
                device_id={"space": left},
                device_id_type=MESH,
            ),
            pltpu.make_async_remote_copy(
                src_ref=high_ref.at[slot],
                dst_ref=from_left.at[slot],
                send_sem=halo_send.at[slot, 1],
                recv_sem=halo_recv.at[slot, 1],
                device_id={"space": right},
                device_id_type=MESH,
            ),
        )

    for copy in halo(0):
        copy.start()

    row_at = lax.broadcasted_iota(jnp.int32, (rows, lanes), 0)
    first_row = row_at == 0
    last_row = row_at == rows - 1
    upper_half = lax.broadcasted_iota(jnp.int32, (8, lanes), 0) < 4
    gain = [float(-2.0 / WEIGHTS[i]) for i in range(4)]

    sub = lax.rem(lax.broadcasted_iota(jnp.int32, (8, lanes), 0), 4)

    def by_node(values):
        return jnp.where(
            sub == 0, values[0], jnp.where(sub == 1, values[1], jnp.where(sub == 2, values[2], values[3]))
        )

    def choose(mask, left, right):
        return tuple(
            tuple(jnp.where(mask, a, b) for a, b in zip(p, q)) for p, q in zip(left, right)
        )

    def lane_rolled(node, shift):
        return rolled(node, shift, 1)

    def coefficient(a, b):
        return float(2.0 * WEIGHTS[a] * DERIVATIVE[a, b])

    side = jnp.where(upper_half, 1.0, -1.0)

    def outside(nodes, edge, blend):
        near = nodes[0]
        high = [0.0] * VARS
        for d in (1, 2, 3):
            term = two_point(nodes[d], near, 0, coefficient(3 - d, 3))
            high = [high[v] + term[v] for v in range(VARS)]
        phys = [physical(nodes[d], 0) for d in (0, 1)]
        fast = [jnp.abs(nodes[d][1][0]) + nodes[d][1][6] for d in (0, 1)]
        speed = side * jnp.maximum(fast[0], fast[1])
        rate = []
        for v in range(VARS):
            low = 0.5 * (phys[0][v] + phys[1][v] - speed * (near[0][v] - nodes[1][0][v]))
            inner = high[v] + blend * (low - high[v])
            rate.append((gain[3] * side) * (edge[v] - inner))

        wrapped = rolled(near, 5, 0)
        before = choose(sub == 0, lane_rolled(wrapped, 1), rolled(near, 1, 0))
        first = two_point(before, near, 1, 1.0)
        second = two_point(choose(sub == 0, wrapped, rolled(near, 2, 0)), near, 1, 1.0)
        first_scale = by_node([0.0, coefficient(0, 1), coefficient(1, 2), coefficient(2, 3)])
        second_scale = by_node([coefficient(0, 3), 0.0, coefficient(0, 2), coefficient(1, 3)])
        before_phys, near_phys = physical(before, 1), physical(near, 1)
        speed = 0.5 * jnp.maximum(
            jnp.abs(before[1][1]) + before[1][6], jnp.abs(near[1][1]) + near[1][6]
        )
        gains = by_node(gain)
        result = []
        for v in range(VARS):
            damping = speed * (near[0][v] - before[0][v])
            far = second_scale * second[v]
            high = first_scale * first[v] + jnp.where(sub >= 2, far, 0.0)
            high = high + jnp.where(
                jnp.logical_or(sub == 1, sub == 2), pltpu.roll(far, 7, 0), 0.0
            )
            high = high + by_node(
                [0.0, pltpu.roll(far, 1, 0), pltpu.roll(far, 2, 0), pltpu.roll(far, 3, 0)]
            )
            low = 0.5 * (before_phys[v] + near_phys[v]) - damping
            wall = jnp.where(sub == 0, first[v] - damping, high + blend * (low - high))
            above = jnp.where(
                sub == 3,
                pltpu.roll(pltpu.roll(wall, 3, 0), lanes - 1, 1),
                pltpu.roll(wall, 7, 0),
            )
            result.append(near[0][v] + step_size * (rate[v] + gains * (above - wall)))
        return result

    def stage(first, slot, src, dst, keep):
        fresh = 1.0 - keep
        fresh_step = fresh * step_size

        def load(i, j):
            u = tuple(src[v, i, j] for v in range(VARS))
            return (u, tuple(fld[k, i, j] for k in range(7)))

        for i in range(4):
            for j in range(4):
                values = node_fields(tuple(src[v, i, j] for v in range(VARS)))
                for k in range(7):
                    fld[k, i, j] = values[k]
        blend = blend_ref[...]

        def across(t):
            nodes = [load(i, t) for i in range(4)]
            inner = line_fluxes(nodes, 0, blend)
            face = face_flux(rolled(nodes[3], 1, 0), nodes[0], 0)
            for v in range(VARS):
                lower = jnp.where(first_row, 0.0, face[v])
                upper = jnp.where(last_row, 0.0, pltpu.roll(face[v], rows - 1, 0))
                walls = [lower, inner[0][v], inner[1][v], inner[2][v], upper]
                for i in range(4):
                    acc[v, i, t] = gain[i] * (walls[i + 1] - walls[i])

        def upward(t):
            nodes = [load(t, j) for j in range(4)]
            inner = line_fluxes(nodes, 1, blend)
            face = face_flux(rolled(nodes[3], 1, 1), nodes[0], 1)
            for v in range(VARS):
                upper = pltpu.roll(face[v], lanes - 1, 1)
                walls = [face[v], inner[0][v], inner[1][v], inner[2][v], upper]
                for j in range(4):
                    total = acc[v, t, j] + gain[j] * (walls[j + 1] - walls[j])
                    value = fresh * nodes[j][0][v] + fresh_step * total
                    if keep:
                        value = value + keep * dst[v, t, j]
                    dst[v, t, j] = value

        for t in range(4):
            across(t)
        for t in (1, 2):
            upward(t)

        if first:
            for copy in halo(slot):
                copy.wait()

            def packed(v, d):
                left_tile = from_left[slot, 2 * v + d // 2]
                right_tile = from_right[slot, 2 * v + d // 2]
                if d % 2:
                    left_tile = pltpu.roll(left_tile, 4, 0)
                else:
                    right_tile = pltpu.roll(right_tile, 4, 0)
                return jnp.where(upper_half, left_tile, right_tile)

            values = [tuple(packed(v, d) for v in range(VARS)) for d in range(4)]
            beyond = [(u, node_fields(u)) for u in values]
            own = tuple(
                jnp.where(upper_half, low_ref[slot, 2 * v], pltpu.roll(high_ref[slot, 2 * v], 4, 0))
                for v in range(VARS)
            )
        else:
            u = tuple(near_ref[v] for v in range(VARS))
            beyond = [(u, node_fields(u))]
            own = tuple(own_ref[v] for v in range(VARS))
        own = (own, node_fields(own))
        edge = face_flux(
            choose(upper_half, beyond[0], own), choose(upper_half, own, beyond[0]), 0
        )
        factor = jnp.where(upper_half, -gain[0] * fresh_step, gain[3] * fresh_step)
        for v in range(VARS):
            edge_ref[v] = factor * edge[v]
        if first:
            outer_blend = jnp.where(
                upper_half, from_left[slot, 2 * VARS], from_right[slot, 2 * VARS]
            )
            stepped = outside(beyond, edge, outer_blend)
            for v in range(VARS):
                near_ref[v] = stepped[v]
        for t in (0, 3):
            upward(t)
        for v in range(VARS):
            for j in range(4):
                low = dst[v, 0, j, 0:1, :] + edge_ref[v, j : j + 1, :]
                high = dst[v, 3, j, rows - 1 : rows, :] + edge_ref[v, 4 + j : 5 + j, :]
                dst[v, 0, j, 0:1, :] = low
                dst[v, 3, j, rows - 1 : rows, :] = high
                if first:
                    own_ref[v, j : j + 1, :] = low
                    own_ref[v, 4 + j : 5 + j, :] = high

    def fine_step(step, _):
        slot = lax.rem(step, 2)
        stage(True, slot, u_ref, w_ref, 0.0)
        stage(False, slot, w_ref, u_ref, 0.5)

        @pl.when(step < FSTEPS - 1)
        def _():
            pack(1 - slot)
            for copy in halo(1 - slot):
                copy.start()

        return 0

    lax.fori_loop(0, FSTEPS, fine_step, 0)

    def grid_of(view):
        return [[view(i, j) for j in range(4)] for i in range(4)]

    def pass_on(src, dst, send, recv, k, device):
        return pltpu.make_async_remote_copy(
            src_ref=src,
            dst_ref=dst,
            send_sem=send.at[k],
            recv_sem=recv.at[k],
            device_id={"tm": device},
            device_id_type=MESH,
        )

    def to_mate(v):
        return pass_on(corr.at[v], mate.at[v], corr_send, corr_recv, v, partner)

    def mean_to_next(v):
        return pass_on(
            mean_out.at[v], mean_in.at[v], chain_send, chain_recv, VARS * 4 + v, tm + 2
        )

    def to_next(v, i):
        return pass_on(
            end_ref.at[0, v, i], start_ref.at[v, i], chain_send, chain_recv, v * 4 + i, tm + 2
        )

    def to_first(v, i):
        return pass_on(
            start_ref.at[v, i], start_ref.at[v, i], fwd_send, fwd_recv, v * 4 + i, partner
        )

    def store(v):
        return pltpu.make_async_copy(end_ref.at[0, v], end_hbm.at[0, v], store_sem.at[v])

    def pair_up(v):
        to_mate(v).wait_recv()
        half = coarse(grid_of(lambda i, j: mate[v, i, j]), fac_ref[v])
        values = [[half[i][j] + corr[v, i, j] for j in range(4)] for i in range(4)]
        mean = None
        for i in range(4):
            for j in range(4):
                term = QUAD[i][j] * values[i][j]
                mean = term if mean is None else mean + term
        return values, mean

    counted = jnp.where(tm == 0, 0.0, 1.0)
    for v in range(VARS):
        base = coarse(grid_of(lambda i, j: o_ref[0, v, i, j]), fac_ref[v])
        for i in range(4):
            for j in range(4):
                corr[v, i, j] = u_ref[v, i, j] - counted * base[i][j]

        @pl.when(core == 0)
        def _():
            to_mate(v).start()

    jump_ref[0] = jnp.zeros((rows, lanes), jnp.float32)

    @pl.when(core == 0)
    def _():
        @pl.when(z == 0)
        def _():
            end_ref[0] = corr[...]
            for v in range(VARS):
                store(v).start()

        @pl.when(z > 0)
        def _():
            total = jnp.zeros((rows, lanes), jnp.float32)
            for v in range(VARS):
                for i in range(4):
                    to_first(v, i).wait_recv()
                begun = grid_of(lambda i, j: start_ref[v, i, j])
                ended = coarse(begun, fac_ref[v])
                for i in range(4):
                    for j in range(4):
                        jump = begun[i][j] - o_ref[0, v, i, j]
                        total = total + QUAD[i][j] * (jump * jump)
                        end_ref[0, v, i, j] = ended[i][j] + corr[v, i, j]
                store(v).start()
            jump_ref[0] = total

    @pl.when(core == 1)
    def _():
        @pl.when(z == 0)
        def _():
            total = jnp.zeros((rows, lanes), jnp.float32)
            for v in range(VARS):
                values, mean = pair_up(v)
                mean_out[v] = mean
                for i in range(4):
                    for j in range(4):
                        end_ref[0, v, i, j] = values[i][j]

                @pl.when(gives)
                def _():
                    mean_to_next(v).start()
                    for i in range(4):
                        to_next(v, i).start()

                store(v).start()
                for i in range(4):
                    for j in range(4):
                        jump = mate[v, i, j] - o_ref[0, v, i, j]
                        total = total + QUAD[i][j] * (jump * jump)
            jump_ref[0] = total

        @pl.when(z > 0)
        def _():
            for v in range(VARS):
                values, mean = pair_up(v)
                mean_out[v] = mean
                for i in range(4):
                    for j in range(4):
                        pairs[v, i, j] = values[i][j]

            total = jnp.zeros((rows, lanes), jnp.float32)
            for v in range(VARS):
                mean_to_next(v).wait_recv()
                mean = mean_in[v]
                mean_out[v] = mean + mean_out[v]

                @pl.when(gives)
                def _():
                    mean_to_next(v).start()

                factor = fac_ref[v]
                twice = factor * factor
                for i in range(4):
                    to_next(v, i).wait_recv()
                    for j in range(4):
                        end_ref[0, v, i, j] = (
                            mean + twice * (start_ref[v, i, j] - mean) + pairs[v, i, j]
                        )

                    @pl.when(gives)
                    def _():
                        to_next(v, i).start()

                    to_first(v, i).start()

                store(v).start()
                begun = coarse(grid_of(lambda i, j: start_ref[v, i, j]), factor)
                for i in range(4):
                    for j in range(4):
                        jump = (begun[i][j] + mate[v, i, j]) - o_ref[0, v, i, j]
                        total = total + QUAD[i][j] * (jump * jump)
            jump_ref[0] = total

    def share(k):
        return pltpu.make_async_remote_copy(
            src_ref=jump_ref.at[0],
            dst_ref=jump_ref.at[k],
            send_sem=jump_send.at[k],
            recv_sem=jump_recv.at[k],
            device_id={"space": lax.rem(sp + k, n_space)},
            device_id_type=MESH,
        )

    for k in range(1, n_space):
        share(k).start()

    @pl.when(core == 0)
    def _():
        for v in range(VARS):
            to_mate(v).wait_send()

    @pl.when(takes)
    def _():
        for v in range(VARS):
            for i in range(4):
                to_first(v, i).wait_send()

    @pl.when(gives)
    def _():
        for v in range(VARS):
            mean_to_next(v).wait_send()
            for i in range(4):
                to_next(v, i).wait_send()

    for v in range(VARS):
        store(v).wait()

    for k in range(1, n_space):
        share(k).wait()
    total = jump_ref[0]
    for k in range(1, n_space):
        total = total + jump_ref[k]
    total = jnp.sum(jnp.sum(total, axis=0, keepdims=True), axis=1, keepdims=True)
    norm_ref[...] = jnp.broadcast_to(
        jnp.sqrt(total * (1.0 / (n_space * rows * lanes))), norm_ref.shape
    )


def solution(mesh):
    n_tm = mesh.shape["tm"]
    n_space = mesh.shape["space"]

    def on_device(slab_starts, coarse_factor, blend_weight, blend_flags):
        rows, lanes = blend_weight.shape
        state = (VARS, NODES, NODES, rows, lanes)
        f32 = jnp.float32
        dma = pltpu.SemaphoreType.DMA
        vmem = pl.BlockSpec(memory_space=pltpu.VMEM)
        edges = pltpu.VMEM((2, 2 * VARS + 1, 8, lanes), f32)
        ends, norm = pl.pallas_call(
            functools.partial(kernel, n_space, n_tm),
            out_shape=(
                jax.ShapeDtypeStruct((1,) + state, f32),
                jax.ShapeDtypeStruct((1, 128), f32),
            ),
            in_specs=[pl.BlockSpec(memory_space=pltpu.HBM)] * 4,
            out_specs=(pl.BlockSpec(memory_space=pltpu.HBM), vmem),
            scratch_shapes=[
                pltpu.VMEM((1,) + state, f32),
                pltpu.VMEM((VARS, rows, lanes), f32),
                pltpu.VMEM((VARS, rows, lanes), f32),
                pltpu.VMEM((1,) + state, f32),
                pltpu.VMEM(coarse_factor.shape, f32),
                pltpu.VMEM(blend_weight.shape, f32),
                pltpu.VMEM(blend_flags.shape, blend_flags.dtype),
                pltpu.VMEM(state, f32),
                pltpu.VMEM(state, f32),
                pltpu.VMEM((7, NODES, NODES, rows, lanes), f32),
                pltpu.VMEM(state, f32),
                pltpu.VMEM((rows, lanes), f32),
                edges,
                edges,
                edges,
                edges,
                pltpu.VMEM((VARS, 8, lanes), f32),
                pltpu.VMEM((VARS, 8, lanes), f32),
                pltpu.VMEM((VARS, 8, lanes), f32),
                pltpu.VMEM(state, f32),
                pltpu.VMEM(state, f32),
                pltpu.VMEM(state, f32),
                pltpu.VMEM(state, f32),
                pltpu.VMEM((n_space, rows, lanes), f32),
                dma((2, 2)),
                dma((2, 2)),
                dma((VARS,)),
                dma((VARS,)),
                dma((VARS * 5,)),
                dma((VARS * 5,)),
                dma((VARS * 4,)),
                dma((VARS * 4,)),
                dma((n_space,)),
                dma((n_space,)),
                dma((4,)),
                dma((VARS,)),
            ],
            compiler_params=pltpu.CompilerParams(
                collective_id=0, has_side_effects=True, vmem_limit_bytes=64 * 1024 * 1024
            ),
        )(slab_starts, coarse_factor, blend_weight, blend_flags)
        return ends, norm[0, :1]

    in_specs = (
        P("tm", None, None, None, "space", None),
        P(None, "space", None),
        P("space", None),
        P("space", None),
    )
    out_specs = (P("tm", None, None, None, "space", None), P("tm"))
    return jax.shard_map(
        on_device, mesh=mesh, in_specs=in_specs, out_specs=out_specs, check_vma=False
    )
```

```python
import functools
import math

import jax
import jax.numpy as jnp
import numpy as np
from jax import lax
from jax.experimental import pallas as pl
from jax.experimental.pallas import tpu as pltpu
from jax.sharding import PartitionSpec as P

FSTEPS = 4
NODES = 4
VARS = 4

gamma_ratio = 1.4
step_size = 0.003
MESH = pl.DeviceIdType.MESH


def tables():
    inner = 1.0 / math.sqrt(5.0)
    points = np.array([-1.0, -inner, inner, 1.0])
    weights = np.array([1.0 / 6.0, 5.0 / 6.0, 5.0 / 6.0, 1.0 / 6.0])
    scales = [
        1.0 / np.prod([points[c] - points[k] for k in range(4) if k != c]) for c in range(4)
    ]
    derivative = np.zeros((4, 4))
    for r in range(4):
        for c in range(4):
            if r != c:
                derivative[r, c] = scales[c] / scales[r] / (points[r] - points[c])
    return derivative, weights


DERIVATIVE, WEIGHTS = tables()
QUAD = [[float(WEIGHTS[i] * WEIGHTS[j] / 4.0) for j in range(4)] for i in range(4)]


def rough(x):
    return pl.reciprocal(x, approx=True)


def inverse(x):
    r = pl.reciprocal(x, approx=True)
    return r * (2.0 - x * r)


def near_terms(a, b):
    total = a + b
    differ = b - a
    ratio = differ * rough(total)
    ratio = ratio * ratio
    series = 2.0 + ratio * (35.0 / 52.5 + ratio * (21.0 / 52.5 + ratio * (15.0 / 52.5)))
    return ratio < 0.0001, total, differ, series


def node_fields(u):
    rho, mx, my, energy = u
    ir = inverse(rho)
    vx = mx * ir
    vy = my * ir
    p = 0.4 * energy - 0.2 * (mx * vx + my * vy)
    beta = rho * inverse(p)
    warm = gamma_ratio * p * ir
    sound = warm * lax.rsqrt(warm)
    return (vx, vy, p, beta, jnp.log(rho), 2.5 * jnp.log(beta), sound)


def two_point(left, right, axis, scale):
    (ul, fl), (ur, fr) = left, right
    vnl, vtl = (fl[0], fl[1]) if axis == 0 else (fl[1], fl[0])
    vnr, vtr = (fr[0], fr[1]) if axis == 0 else (fr[1], fr[0])
    near, total, differ, series = near_terms(ul[0], ur[0])
    mean = jnp.where(near, total, differ) * inverse(jnp.where(near, series, fr[4] - fl[4]))
    near, total, differ, series = near_terms(fl[3], fr[3])
    thermal = jnp.where(near, 2.5 * series, fr[5] - fl[5]) * inverse(
        jnp.where(near, total, differ)
    )
    half_n = 0.5 * (vnl + vnr)
    half_t = 0.5 * (vtl + vtr)
    mass = mean * half_n
    if scale != 1.0:
        mass = mass * scale
    normal = mass * half_n + (0.5 * scale) * (fl[2] + fr[2])
    along = mass * half_t
    energy = mass * (0.5 * (vnl * vnr + vtl * vtr) + thermal) + (0.5 * scale) * (
        fl[2] * vnr + fr[2] * vnl
    )
    return (mass, normal, along, energy) if axis == 0 else (mass, along, normal, energy)


def face_flux(left, right, axis):
    (ul, fl), (ur, fr) = left, right
    centre = two_point(left, right, axis, 1.0)
    speed = 0.5 * jnp.maximum(jnp.abs(fl[axis]) + fl[6], jnp.abs(fr[axis]) + fr[6])
    return [centre[v] - speed * (ur[v] - ul[v]) for v in range(VARS)]


def physical(node, axis):
    u, f = node
    vn = f[axis]
    flux = [u[0] * vn, u[1] * vn, u[2] * vn, (u[3] + f[2]) * vn]
    flux[0] = u[1 + axis]
    flux[1 + axis] = flux[1 + axis] + f[2]
    return flux


def line_fluxes(nodes, axis, blend):
    pair = {}
    for a in range(4):
        for b in range(a + 1, 4):
            weight = float(2.0 * WEIGHTS[a] * DERIVATIVE[a, b])
            pair[a, b] = two_point(nodes[a], nodes[b], axis, weight)
    phys = [physical(node, axis) for node in nodes]
    fast = [jnp.abs(node[1][axis]) + node[1][6] for node in nodes]
    speeds = [jnp.maximum(fast[k], fast[k + 1]) for k in range(3)]
    result = [[], [], []]
    for v in range(VARS):
        far = pair[0, 3][v]
        head = pair[0, 2][v] + far
        tail = pair[1, 3][v]
        high = [pair[0, 1][v] + head, head + (pair[1, 2][v] + tail), (far + tail) + pair[2, 3][v]]
        for k in range(3):
            low = 0.5 * (
                (phys[k][v] + phys[k + 1][v])
                - speeds[k] * (nodes[k + 1][0][v] - nodes[k][0][v])
            )
            result[k].append(high[k] + blend * (low - high[k]))
    return result


def rolled(node, shift, axis):
    return tuple(tuple(pltpu.roll(x, shift, axis) for x in part) for part in node)


def coarse(u, factor):
    mean = None
    for i in range(4):
        for j in range(4):
            term = QUAD[i][j] * u[i][j]
            mean = term if mean is None else mean + term
    return [[mean + factor * (u[i][j] - mean) for j in range(4)] for i in range(4)]


def kernel(
    n_space,
    n_tm,
    o_hbm,
    fac_hbm,
    bw_hbm,
    bf_hbm,
    end_hbm,
    norm_ref,
    end_ref,
    mean_in,
    mean_out,
    o_ref,
    fac_ref,
    bw_ref,
    bf_ref,
    u_ref,
    w_ref,
    fld,
    acc,
    blend_ref,
    low_ref,
    high_ref,
    from_left,
    from_right,
    edge_ref,
    own_ref,
    near_ref,
    corr,
    mate,
    pairs,
    start_ref,
    jump_ref,
    halo_send,
    halo_recv,
    corr_send,
    corr_recv,
    chain_send,
    chain_recv,
    fwd_send,
    fwd_recv,
    jump_send,
    jump_recv,
    load_sem,
    store_sem,
):
    rows, lanes = bw_ref.shape
    loads = [
        pltpu.make_async_copy(src, dst, load_sem.at[k])
        for k, (src, dst) in enumerate(
            ((o_hbm, o_ref), (fac_hbm, fac_ref), (bw_hbm, bw_ref), (bf_hbm, bf_ref))
        )
    ]
    for copy in loads:
        copy.start()
    sp = lax.axis_index("space")
    tm = lax.axis_index("tm")
    core = lax.rem(tm, 2)
    z = lax.div(tm, 2)
    partner = tm + 1 - 2 * core
    chips = n_tm // 2
    left = lax.rem(sp + n_space - 1, n_space)
    right = lax.rem(sp + 1, n_space)
    takes = jnp.logical_and(core == 1, z > 0)
    gives = jnp.logical_and(core == 1, z < chips - 1)

    barrier = pltpu.get_barrier_semaphore()
    for k in range(1, n_space):
        other = lax.rem(sp + k, n_space)
        pl.semaphore_signal(barrier, inc=1, device_id={"space": other}, device_id_type=MESH)
    pl.semaphore_signal(barrier, inc=1, device_id={"tm": partner}, device_id_type=MESH)

    @pl.when(takes)
    def _():
        pl.semaphore_signal(barrier, inc=1, device_id={"tm": tm - 2}, device_id_type=MESH)

    @pl.when(gives)
    def _():
        pl.semaphore_signal(barrier, inc=1, device_id={"tm": tm + 2}, device_id_type=MESH)

    for copy in loads:
        copy.wait()
    blend_ref[...] = bf_ref[...].astype(jnp.float32) * bw_ref[...]
    for slot in range(2):
        low_ref[slot, 2 * VARS] = jnp.broadcast_to(blend_ref[0:1, :], (8, lanes))
        high_ref[slot, 2 * VARS] = jnp.broadcast_to(blend_ref[rows - 1 : rows, :], (8, lanes))

    def pack(slot):
        for v in range(VARS):
            for d in range(4):
                for j in range(4):
                    at = 4 * (d % 2) + j
                    low_ref[slot, 2 * v + d // 2, at : at + 1, :] = u_ref[v, d, j, 0:1, :]
                    high_ref[slot, 2 * v + d // 2, at : at + 1, :] = u_ref[
                        v, 3 - d, j, rows - 1 : rows, :
                    ]

    u_ref[...] = o_ref[0]
    pack(0)

    peers = n_space + takes.astype(jnp.int32) + gives.astype(jnp.int32)
    pl.semaphore_wait(barrier, peers)

    def halo(slot):
        return (
            pltpu.make_async_remote_copy(
                src_ref=low_ref.at[slot],
                dst_ref=from_right.at[slot],
                send_sem=halo_send.at[slot, 0],
                recv_sem=halo_recv.at[slot, 0],
                device_id={"space": left},
                device_id_type=MESH,
            ),
            pltpu.make_async_remote_copy(
                src_ref=high_ref.at[slot],
                dst_ref=from_left.at[slot],
                send_sem=halo_send.at[slot, 1],
                recv_sem=halo_recv.at[slot, 1],
                device_id={"space": right},
                device_id_type=MESH,
            ),
        )

    for copy in halo(0):
        copy.start()

    row_at = lax.broadcasted_iota(jnp.int32, (rows, lanes), 0)
    first_row = row_at == 0
    last_row = row_at == rows - 1
    upper_half = lax.broadcasted_iota(jnp.int32, (8, lanes), 0) < 4
    gain = [float(-2.0 / WEIGHTS[i]) for i in range(4)]

    sub = lax.rem(lax.broadcasted_iota(jnp.int32, (8, lanes), 0), 4)

    def by_node(values):
        return jnp.where(
            sub == 0, values[0], jnp.where(sub == 1, values[1], jnp.where(sub == 2, values[2], values[3]))
        )

    def choose(mask, left, right):
        return tuple(
            tuple(jnp.where(mask, a, b) for a, b in zip(p, q)) for p, q in zip(left, right)
        )

    def lane_rolled(node, shift):
        return rolled(node, shift, 1)

    def coefficient(a, b):
        return float(2.0 * WEIGHTS[a] * DERIVATIVE[a, b])

    side = jnp.where(upper_half, 1.0, -1.0)

    def outside(nodes, edge, blend):
        near = nodes[0]
        high = [0.0] * VARS
        for d in (1, 2, 3):
            term = two_point(nodes[d], near, 0, coefficient(3 - d, 3))
            high = [high[v] + term[v] for v in range(VARS)]
        phys = [physical(nodes[d], 0) for d in (0, 1)]
        fast = [jnp.abs(nodes[d][1][0]) + nodes[d][1][6] for d in (0, 1)]
        speed = side * jnp.maximum(fast[0], fast[1])
        rate = []
        for v in range(VARS):
            low = 0.5 * (phys[0][v] + phys[1][v] - speed * (near[0][v] - nodes[1][0][v]))
            inner = high[v] + blend * (low - high[v])
            rate.append((gain[3] * side) * (edge[v] - inner))

        wrapped = rolled(near, 5, 0)
        before = choose(sub == 0, lane_rolled(wrapped, 1), rolled(near, 1, 0))
        first = two_point(before, near, 1, 1.0)
        second = two_point(choose(sub == 0, wrapped, rolled(near, 2, 0)), near, 1, 1.0)
        first_scale = by_node([0.0, coefficient(0, 1), coefficient(1, 2), coefficient(2, 3)])
        second_scale = by_node([coefficient(0, 3), 0.0, coefficient(0, 2), coefficient(1, 3)])
        before_phys, near_phys = physical(before, 1), physical(near, 1)
        speed = 0.5 * jnp.maximum(
            jnp.abs(before[1][1]) + before[1][6], jnp.abs(near[1][1]) + near[1][6]
        )
        gains = by_node(gain)
        result = []
        for v in range(VARS):
            damping = speed * (near[0][v] - before[0][v])
            far = second_scale * second[v]
            high = first_scale * first[v] + jnp.where(sub >= 2, far, 0.0)
            high = high + jnp.where(
                jnp.logical_or(sub == 1, sub == 2), pltpu.roll(far, 7, 0), 0.0
            )
            high = high + by_node(
                [0.0, pltpu.roll(far, 1, 0), pltpu.roll(far, 2, 0), pltpu.roll(far, 3, 0)]
            )
            low = 0.5 * (before_phys[v] + near_phys[v]) - damping
            wall = jnp.where(sub == 0, first[v] - damping, high + blend * (low - high))
            above = jnp.where(
                sub == 3,
                pltpu.roll(pltpu.roll(wall, 3, 0), lanes - 1, 1),
                pltpu.roll(wall, 7, 0),
            )
            result.append(near[0][v] + step_size * (rate[v] + gains * (above - wall)))
        return result

    def stage(first, slot, src, dst, keep):
        fresh = 1.0 - keep
        fresh_step = fresh * step_size

        def load(i, j):
            u = tuple(src[v, i, j] for v in range(VARS))
            return (u, tuple(fld[k, i, j] for k in range(7)))

        for i in range(4):
            for j in range(4):
                values = node_fields(tuple(src[v, i, j] for v in range(VARS)))
                for k in range(7):
                    fld[k, i, j] = values[k]
        blend = blend_ref[...]

        def across(t):
            nodes = [load(i, t) for i in range(4)]
            inner = line_fluxes(nodes, 0, blend)
            face = face_flux(rolled(nodes[3], 1, 0), nodes[0], 0)
            for v in range(VARS):
                lower = jnp.where(first_row, 0.0, face[v])
                upper = jnp.where(last_row, 0.0, pltpu.roll(face[v], rows - 1, 0))
                walls = [lower, inner[0][v], inner[1][v], inner[2][v], upper]
                for i in range(4):
                    acc[v, i, t] = gain[i] * (walls[i + 1] - walls[i])

        def upward(t):
            nodes = [load(t, j) for j in range(4)]
            inner = line_fluxes(nodes, 1, blend)
            face = face_flux(rolled(nodes[3], 1, 1), nodes[0], 1)
            for v in range(VARS):
                upper = pltpu.roll(face[v], lanes - 1, 1)
                walls = [face[v], inner[0][v], inner[1][v], inner[2][v], upper]
                for j in range(4):
                    total = acc[v, t, j] + gain[j] * (walls[j + 1] - walls[j])
                    value = fresh * nodes[j][0][v] + fresh_step * total
                    if keep:
                        value = value + keep * dst[v, t, j]
                    dst[v, t, j] = value

        def across_step(t, _):
            across(t)
            return 0

        lax.fori_loop(0, 4, across_step, 0)
        for t in (1, 2):
            upward(t)

        if first:
            for copy in halo(slot):
                copy.wait()

            def packed(v, d):
                left_tile = from_left[slot, 2 * v + d // 2]
                right_tile = from_right[slot, 2 * v + d // 2]
                if d % 2:
                    left_tile = pltpu.roll(left_tile, 4, 0)
                else:
                    right_tile = pltpu.roll(right_tile, 4, 0)
                return jnp.where(upper_half, left_tile, right_tile)

            values = [tuple(packed(v, d) for v in range(VARS)) for d in range(4)]
            beyond = [(u, node_fields(u)) for u in values]
            own = tuple(
                jnp.where(upper_half, low_ref[slot, 2 * v], pltpu.roll(high_ref[slot, 2 * v], 4, 0))
                for v in range(VARS)
            )
        else:
            u = tuple(near_ref[v] for v in range(VARS))
            beyond = [(u, node_fields(u))]
            own = tuple(own_ref[v] for v in range(VARS))
        own = (own, node_fields(own))
        edge = face_flux(
            choose(upper_half, beyond[0], own), choose(upper_half, own, beyond[0]), 0
        )
        factor = jnp.where(upper_half, -gain[0] * fresh_step, gain[3] * fresh_step)
        for v in range(VARS):
            edge_ref[v] = factor * edge[v]
        if first:
            outer_blend = jnp.where(
                upper_half, from_left[slot, 2 * VARS], from_right[slot, 2 * VARS]
            )
            stepped = outside(beyond, edge, outer_blend)
            for v in range(VARS):
                near_ref[v] = stepped[v]
        for t in (0, 3):
            upward(t)
        for v in range(VARS):
            for j in range(4):
                low = dst[v, 0, j, 0:1, :] + edge_ref[v, j : j + 1, :]
                high = dst[v, 3, j, rows - 1 : rows, :] + edge_ref[v, 4 + j : 5 + j, :]
                dst[v, 0, j, 0:1, :] = low
                dst[v, 3, j, rows - 1 : rows, :] = high
                if first:
                    own_ref[v, j : j + 1, :] = low
                    own_ref[v, 4 + j : 5 + j, :] = high

    def fine_step(step, _):
        slot = lax.rem(step, 2)
        stage(True, slot, u_ref, w_ref, 0.0)
        stage(False, slot, w_ref, u_ref, 0.5)

        @pl.when(step < FSTEPS - 1)
        def _():
            pack(1 - slot)
            for copy in halo(1 - slot):
                copy.start()

        return 0

    lax.fori_loop(0, FSTEPS, fine_step, 0)

    def grid_of(view):
        return [[view(i, j) for j in range(4)] for i in range(4)]

    def pass_on(src, dst, send, recv, k, device):
        return pltpu.make_async_remote_copy(
            src_ref=src,
            dst_ref=dst,
            send_sem=send.at[k],
            recv_sem=recv.at[k],
            device_id={"tm": device},
            device_id_type=MESH,
        )

    def to_mate(v):
        return pass_on(corr.at[v], mate.at[v], corr_send, corr_recv, v, partner)

    def mean_to_next(v):
        return pass_on(
            mean_out.at[v], mean_in.at[v], chain_send, chain_recv, VARS * 4 + v, tm + 2
        )

    def to_next(v, i):
        return pass_on(
            end_ref.at[0, v, i], start_ref.at[v, i], chain_send, chain_recv, v * 4 + i, tm + 2
        )

    def to_first(v, i):
        return pass_on(
            start_ref.at[v, i], start_ref.at[v, i], fwd_send, fwd_recv, v * 4 + i, partner
        )

    def store(v):
        return pltpu.make_async_copy(end_ref.at[0, v], end_hbm.at[0, v], store_sem.at[v])

    def pair_up(v):
        to_mate(v).wait_recv()
        half = coarse(grid_of(lambda i, j: mate[v, i, j]), fac_ref[v])
        values = [[half[i][j] + corr[v, i, j] for j in range(4)] for i in range(4)]
        mean = None
        for i in range(4):
            for j in range(4):
                term = QUAD[i][j] * values[i][j]
                mean = term if mean is None else mean + term
        return values, mean

    counted = jnp.where(tm == 0, 0.0, 1.0)
    for v in range(VARS):
        base = coarse(grid_of(lambda i, j: o_ref[0, v, i, j]), fac_ref[v])
        for i in range(4):
            for j in range(4):
                corr[v, i, j] = u_ref[v, i, j] - counted * base[i][j]

        @pl.when(core == 0)
        def _():
            to_mate(v).start()

    jump_ref[0] = jnp.zeros((rows, lanes), jnp.float32)

    @pl.when(core == 0)
    def _():
        @pl.when(z == 0)
        def _():
            end_ref[0] = corr[...]
            for v in range(VARS):
                store(v).start()

        @pl.when(z > 0)
        def _():
            total = jnp.zeros((rows, lanes), jnp.float32)
            for v in range(VARS):
                for i in range(4):
                    to_first(v, i).wait_recv()
                begun = grid_of(lambda i, j: start_ref[v, i, j])
                ended = coarse(begun, fac_ref[v])
                for i in range(4):
                    for j in range(4):
                        jump = begun[i][j] - o_ref[0, v, i, j]
                        total = total + QUAD[i][j] * (jump * jump)
                        end_ref[0, v, i, j] = ended[i][j] + corr[v, i, j]
                store(v).start()
            jump_ref[0] = total

    @pl.when(core == 1)
    def _():
        @pl.when(z == 0)
        def _():
            total = jnp.zeros((rows, lanes), jnp.float32)
            for v in range(VARS):
                values, mean = pair_up(v)
                mean_out[v] = mean
                for i in range(4):
                    for j in range(4):
                        end_ref[0, v, i, j] = values[i][j]

                @pl.when(gives)
                def _():
                    mean_to_next(v).start()
                    for i in range(4):
                        to_next(v, i).start()

                store(v).start()
                for i in range(4):
                    for j in range(4):
                        jump = mate[v, i, j] - o_ref[0, v, i, j]
                        total = total + QUAD[i][j] * (jump * jump)
            jump_ref[0] = total

        @pl.when(z > 0)
        def _():
            for v in range(VARS):
                values, mean = pair_up(v)
                mean_out[v] = mean
                for i in range(4):
                    for j in range(4):
                        pairs[v, i, j] = values[i][j]

            total = jnp.zeros((rows, lanes), jnp.float32)
            for v in range(VARS):
                mean_to_next(v).wait_recv()
                mean = mean_in[v]
                mean_out[v] = mean + mean_out[v]

                @pl.when(gives)
                def _():
                    mean_to_next(v).start()

                factor = fac_ref[v]
                twice = factor * factor
                for i in range(4):
                    to_next(v, i).wait_recv()
                    for j in range(4):
                        end_ref[0, v, i, j] = (
                            mean + twice * (start_ref[v, i, j] - mean) + pairs[v, i, j]
                        )

                    @pl.when(gives)
                    def _():
                        to_next(v, i).start()

                    to_first(v, i).start()

                store(v).start()
                begun = coarse(grid_of(lambda i, j: start_ref[v, i, j]), factor)
                for i in range(4):
                    for j in range(4):
                        jump = (begun[i][j] + mate[v, i, j]) - o_ref[0, v, i, j]
                        total = total + QUAD[i][j] * (jump * jump)
            jump_ref[0] = total

    def share(k):
        return pltpu.make_async_remote_copy(
            src_ref=jump_ref.at[0],
            dst_ref=jump_ref.at[k],
            send_sem=jump_send.at[k],
            recv_sem=jump_recv.at[k],
            device_id={"space": lax.rem(sp + k, n_space)},
            device_id_type=MESH,
        )

    for k in range(1, n_space):
        share(k).start()

    @pl.when(core == 0)
    def _():
        for v in range(VARS):
            to_mate(v).wait_send()

    @pl.when(takes)
    def _():
        for v in range(VARS):
            for i in range(4):
                to_first(v, i).wait_send()

    @pl.when(gives)
    def _():
        for v in range(VARS):
            mean_to_next(v).wait_send()
            for i in range(4):
                to_next(v, i).wait_send()

    for v in range(VARS):
        store(v).wait()

    for k in range(1, n_space):
        share(k).wait()
    total = jump_ref[0]
    for k in range(1, n_space):
        total = total + jump_ref[k]
    total = jnp.sum(jnp.sum(total, axis=0, keepdims=True), axis=1, keepdims=True)
    norm_ref[...] = jnp.broadcast_to(
        jnp.sqrt(total * (1.0 / (n_space * rows * lanes))), norm_ref.shape
    )


def solution(mesh):
    n_tm = mesh.shape["tm"]
    n_space = mesh.shape["space"]

    def on_device(slab_starts, coarse_factor, blend_weight, blend_flags):
        rows, lanes = blend_weight.shape
        state = (VARS, NODES, NODES, rows, lanes)
        f32 = jnp.float32
        dma = pltpu.SemaphoreType.DMA
        vmem = pl.BlockSpec(memory_space=pltpu.VMEM)
        edges = pltpu.VMEM((2, 2 * VARS + 1, 8, lanes), f32)
        ends, norm = pl.pallas_call(
            functools.partial(kernel, n_space, n_tm),
            out_shape=(
                jax.ShapeDtypeStruct((1,) + state, f32),
                jax.ShapeDtypeStruct((1, 128), f32),
            ),
            in_specs=[pl.BlockSpec(memory_space=pltpu.HBM)] * 4,
            out_specs=(pl.BlockSpec(memory_space=pltpu.HBM), vmem),
            scratch_shapes=[
                pltpu.VMEM((1,) + state, f32),
                pltpu.VMEM((VARS, rows, lanes), f32),
                pltpu.VMEM((VARS, rows, lanes), f32),
                pltpu.VMEM((1,) + state, f32),
                pltpu.VMEM(coarse_factor.shape, f32),
                pltpu.VMEM(blend_weight.shape, f32),
                pltpu.VMEM(blend_flags.shape, blend_flags.dtype),
                pltpu.VMEM(state, f32),
                pltpu.VMEM(state, f32),
                pltpu.VMEM((7, NODES, NODES, rows, lanes), f32),
                pltpu.VMEM(state, f32),
                pltpu.VMEM((rows, lanes), f32),
                edges,
                edges,
                edges,
                edges,
                pltpu.VMEM((VARS, 8, lanes), f32),
                pltpu.VMEM((VARS, 8, lanes), f32),
                pltpu.VMEM((VARS, 8, lanes), f32),
                pltpu.VMEM(state, f32),
                pltpu.VMEM(state, f32),
                pltpu.VMEM(state, f32),
                pltpu.VMEM(state, f32),
                pltpu.VMEM((n_space, rows, lanes), f32),
                dma((2, 2)),
                dma((2, 2)),
                dma((VARS,)),
                dma((VARS,)),
                dma((VARS * 5,)),
                dma((VARS * 5,)),
                dma((VARS * 4,)),
                dma((VARS * 4,)),
                dma((n_space,)),
                dma((n_space,)),
                dma((4,)),
                dma((VARS,)),
            ],
            compiler_params=pltpu.CompilerParams(
                collective_id=0, has_side_effects=True, vmem_limit_bytes=64 * 1024 * 1024
            ),
        )(slab_starts, coarse_factor, blend_weight, blend_flags)
        return ends, norm[0, :1]

    in_specs = (
        P("tm", None, None, None, "space", None),
        P(None, "space", None),
        P("space", None),
        P("space", None),
    )
    out_specs = (P("tm", None, None, None, "space", None), P("tm"))
    return jax.shard_map(
        on_device, mesh=mesh, in_specs=in_specs, out_specs=out_specs, check_vma=False
    )
```
